512 devices in a mesh: doc: 32 (over x, y), leaf: 16 (over z, core).
Axes of the slice: x: 4, y: 8, z: 8, core: 2. Of those that a mesh axis runs over, the one named last changes fastest.
Arguments:
- docs: bfloat16 [16384, 768], P('doc', 'leaf'), may hold values from -6 to 6
- centroids: bfloat16 [32768, 768], P('leaf', 'doc'), may hold values from -6 to 6
Outputs:
- residual_rows: bfloat16 [16384, 768], P('doc', 'leaf')
- leaf_means: bfloat16 [32768, 768], P('leaf', 'doc')
The draws below stay inside these ranges and needn't reach their ends.
All inputs are finite; a program needn't handle non-finite values.
Results may differ from the reference program's by a relative error of at most 0.015.
Values may be sent and summed in bfloat16 or wider, within the bound.
A program may use at most 64 MiB of HBM per device.

```python
import jax
import jax.numpy as jnp
from jax import lax

E = 768
DOCUMENTS_LOCAL = 512
LEAF_DEV = 2048
DOCS = 16384
LEAVES = 32768
N_DOC = 32
N_LEAF = 16


def shared_directions(key):
    block_count = LEAVES // LEAF_DEV
    return jax.random.normal(jax.random.fold_in(key, 101), (block_count, E), jnp.float32)


def draw_docs(key, part):
    directions = shared_directions(key)
    key = jax.random.fold_in(key, 3)
    subkeys = jax.random.split(key, 3)
    block_count = LEAVES // LEAF_DEV
    doc_groups = DOCS // DOCUMENTS_LOCAL
    loadings = jax.random.uniform(subkeys[0], (doc_groups, block_count), jnp.float32, 0.0, 1.0)
    jitter = jax.random.uniform(subkeys[1], (DOCS, block_count), jnp.float32, 0.5, 1.5)
    spread_loadings = jnp.broadcast_to(loadings[:, None, :], (doc_groups, DOCUMENTS_LOCAL, block_count)).reshape(DOCS, block_count)
    weights = spread_loadings * jitter
    base_part = jax.random.normal(subkeys[2], (DOCS, E), jnp.float32)
    weights = 0.6 * weights
    combined = base_part
    for column in range(block_count):
        combined = combined + weights[:, column:column + 1] * directions[column][None, :]
    return jnp.clip(combined, -6.0, 6.0).astype(jnp.bfloat16)


def draw_centroids(key, part):
    directions = shared_directions(key)
    key = jax.random.fold_in(key, 5)
    subkeys = jax.random.split(key, 1)
    block_count = LEAVES // LEAF_DEV
    leaf_direction = jnp.broadcast_to(directions[:, None, :], (block_count, LEAF_DEV, E)).reshape(LEAVES, E)
    base_part = jax.random.normal(subkeys[0], (LEAVES, E), jnp.float32)
    combined = base_part + leaf_direction
    return jnp.clip(combined, -6.0, 6.0).astype(jnp.bfloat16)


def setup_inputs(seed: int = 0) -> dict:
    arg_keys = jax.random.split(jax.random.key(seed), 3)
    docs = draw_docs(jax.random.fold_in(arg_keys[2], 71), 0)
    centroids = draw_centroids(jax.random.fold_in(arg_keys[2], 71), 0)
    return dict(docs=docs, centroids=centroids)


def reference(docs, centroids):
    input_single_float = docs.astype(jnp.float32)
    approximate_input = (input_single_float / jnp.sqrt(lax.optimization_barrier(jnp.mean(input_single_float * input_single_float, axis=1, keepdims=True)) + 1e-06)).astype(jnp.bfloat16)
    c32 = centroids.astype(jnp.float32)
    cnorm = jnp.sqrt(lax.optimization_barrier(jnp.mean(c32 * c32, axis=1)) + 1e-06)
    match_scores = lax.dot_general(approximate_input, centroids, (((1,), (1,)), ((), ())), preferred_element_type=jnp.float32)
    kernel = jnp.exp(match_scores / (E * 0.02 * cnorm)[None, :])
    scales_v = jnp.ones((LEAVES,), jnp.float32)
    scales_u = jnp.ones((DOCS,), jnp.float32)
    for step in range(2):
        scales_u = 1.0 / jnp.dot(kernel, scales_v, precision=lax.Precision.HIGHEST)
        scales_v = DOCS / LEAVES / jnp.dot(scales_u, kernel, precision=lax.Precision.HIGHEST)
    plan = (scales_u[:, None] * kernel * scales_v[None, :]).astype(jnp.bfloat16)
    plan_cols = plan.reshape(DOCS, N_LEAF, LEAF_DEV)
    cent_blocks = centroids.reshape(N_LEAF, LEAF_DEV, E)

    def leaf_step(total, index):
        block = lax.dynamic_index_in_dim(plan_cols, index, 1, keepdims=False)
        part = jnp.dot(block, cent_blocks[index], preferred_element_type=jnp.float32).astype(jnp.bfloat16)
        part = lax.optimization_barrier(part)
        return (total + part.astype(jnp.float32), None)
    recon, _ = lax.scan(leaf_step, jnp.zeros((DOCS, E), jnp.float32), jnp.arange(N_LEAF, dtype=jnp.int32))
    residual_rows = (input_single_float - recon).astype(jnp.bfloat16)
    plan_rows = plan.reshape(N_DOC, DOCUMENTS_LOCAL, LEAVES)
    doc_blocks = docs.reshape(N_DOC, DOCUMENTS_LOCAL, E)

    def doc_step(total, index):
        part = lax.dot_general(plan_rows[index], doc_blocks[index], (((0,), (0,)), ((), ())), preferred_element_type=jnp.float32).astype(jnp.bfloat16)
        part = lax.optimization_barrier(part)
        return (total + part.astype(jnp.float32), None)
    sums, _ = lax.scan(doc_step, jnp.zeros((LEAVES, E), jnp.float32), jnp.arange(N_DOC, dtype=jnp.int32))
    leaf_means = (sums * (LEAVES / DOCS)).astype(jnp.bfloat16)
    return (residual_rows, leaf_means)
```

```python
import jax
import jax.numpy as jnp
from jax import lax
from jax.experimental import pallas as pl
from jax.experimental.pallas import tpu as pltpu
from jax.sharding import PartitionSpec as P

MESH = pl.DeviceIdType.MESH
F32 = jnp.float32
BF16 = jnp.bfloat16

E = 768
NX, NY, NZ, NL = 4, 8, 8, 16
FD, FL = 24, 48
ND, NV = 512, 2048
Q = 512
RATIO = 0.5

YSEQ = (0, -1, 1, -2, 2, -3, 3, -4)
XSEQ = (0, -1, 1, 2)


def kernel(
    docs_ref, cent_ref, res_ref, means_ref,
    dg, ca, cb, ct, xn, dt, kk, ww, ss, rr, ub, pbuf, ybuf, xbuf,
    gs, oa, ob, ra1, ra2, ray, rby, rbx, qq, rq, hq, sq, vv,
    d_send, d_recv, f_send, f_recv,
    ay_send, ay_recv, ax_send, ax_recv, af_send, af_recv,
    bx_send, bx_recv, by_send, by_recv,
    p_send, p_recv, y_send, y_recv, x_send, x_recv,
    rb_send, rb_recv, rbx_send, rbx_recv,
    ra1_send, ra1_recv, ra2_send, ra2_recv, ray_send, ray_recv,
    q1_send, q1_recv, q2_send, q2_recv,
):
    d = lax.axis_index("doc")
    l = lax.axis_index("leaf")
    x, y = lax.div(d, NY), lax.rem(d, NY)
    z, c = lax.div(l, 2), lax.rem(l, 2)

    def at_x(o):
        return lax.rem(x + o + NX, NX)

    def at_y(o):
        return lax.rem(y + o + NY, NY)

    def dev(ox, oy):
        return (at_x(ox) * NY + at_y(oy), l)

    def dev_leaf(zz, cc):
        return (d, zz * 2 + cc)

    other = dev_leaf(z, 1 - c)

    def copy(src, dst, s, r, to):
        return pltpu.make_async_remote_copy(
            src_ref=src, dst_ref=dst, send_sem=s, recv_sem=r, device_id=to, device_id_type=MESH
        )

    def took(ref, sem):
        pltpu.make_async_copy(ref, ref, sem).wait()

    barrier = pltpu.get_barrier_semaphore()

    def greet(to):
        pl.semaphore_signal(barrier, inc=1, device_id=to, device_id_type=MESH)

    def greet_leaf(i, _):
        greet((d, lax.rem(l + i, NL)))
        return 0

    def greet_y(i, _):
        greet((x * NY + lax.rem(y + i, NY), l))
        return 0

    def greet_x(i, _):
        greet((lax.rem(x + i, NX) * NY + y, l))
        return 0

    lax.fori_loop(1, NL, greet_leaf, 0)
    lax.fori_loop(1, NY, greet_y, 0)
    lax.fori_loop(1, NX, greet_x, 0)

    c32 = cent_ref[...].astype(F32)
    ca[x, y] = jnp.concatenate([c32[:, 0:Q], c32[:, Q:2 * Q]], axis=0).astype(BF16)
    cb[y, x] = jnp.concatenate([c32[:, 2 * Q:3 * Q], c32[:, 3 * Q:4 * Q]], axis=0).astype(BF16)
    dg[z, c] = docs_ref[...]

    pl.semaphore_wait(barrier, NL - 1 + NY - 1 + NX - 1)

    def ay(way, step, o):
        ref = ca.at[x, at_y(o)]
        return copy(ref, ref, ay_send.at[way, step], ay_recv.at[way, step], dev(0, 1 if way == 0 else -1))

    def ax(k, way, ox=0):
        ref = ca.at[at_x(ox), at_y(YSEQ[k])]
        return copy(ref, ref, ax_send.at[k, way], ax_recv.at[k, way], dev(1 if way == 0 else -1, 0))

    def af(k, ox):
        ref = ca.at[at_x(ox), at_y(YSEQ[k])]
        return copy(ref, ref, af_send.at[k], af_recv.at[k], dev(1 if k % 2 == 0 else -1, 0))

    def bx(m, ox):
        ref = cb.at[y, at_x(ox)]
        return copy(ref, ref, bx_send.at[m], bx_recv.at[m], dev(-1 if m == 1 else 1, 0))

    def by(way, step, m, o):
        ref = cb.at[at_y(o), at_x(XSEQ[m])]
        return copy(
            ref, ref, by_send.at[way, step, m], by_recv.at[way, step, m], dev(0, 1 if way == 0 else -1)
        )

    def start_ax(k):
        ax(k, 0).start()
        ax(k, 1).start()

    def start_by(m):
        by(0, 0, m, 0).start()
        by(1, 0, m, 0).start()

    def step_ay(s):
        ay(0, s - 1, -s).wait_recv()
        if s < 4:
            ay(0, s, -s).start()
        start_ax(YSEQ.index(-s))
        if s < 4:
            ay(1, s - 1, s).wait_recv()
            if s < 3:
                ay(1, s, s).start()
            start_ax(YSEQ.index(s))

    def step_by(s):
        for m in range(4):
            if s < 4 or m < 2:
                by(0, s - 1, m, -s).wait_recv()
                if s < 3 or (s == 3 and m < 2):
                    by(0, s, m, -s).start()
            if s < 4 or m >= 2:
                by(1, s - 1, m, s).wait_recv()
                if s < 3 or (s == 3 and m >= 2):
                    by(1, s, m, s).start()

    def step_ax(k):
        ax(k, 0, -1).wait_recv()
        if k % 2 == 0:
            af(k, -1).start()
        ax(k, 1, 1).wait_recv()
        if k % 2 == 1:
            af(k, 1).start()

    ay(0, 0, 0).start()
    ay(1, 0, 0).start()
    start_ax(0)
    bx(0, 0).start()
    bx(1, 0).start()
    start_by(0)

    def send_docs(i, _):
        zz = lax.rem(z + i, NZ)
        copy(dg.at[z, c], dg.at[z, c], d_send, d_recv.at[NZ - i], dev_leaf(zz, c)).start()
        return 0

    lax.fori_loop(1, NZ, send_docs, 0)
    copy(dg.at[z, c], dg.at[z, c], f_send, f_recv, other).start()

    step_ay(1)
    bx(0, -1).wait_recv()
    bx(2, -1).start()
    start_by(1)
    bx(1, 1).wait_recv()
    start_by(2)
    step_ay(2)
    bx(2, 2).wait_recv()
    start_by(3)
    step_ax(0)
    step_by(1)
    step_ay(3)
    step_ax(1)
    step_ax(2)
    step_by(2)
    step_ay(4)
    step_ax(3)
    step_ax(4)

    def pass_docs(i, _):
        zz = lax.rem(z + i, NZ)
        ref = dg.at[zz, c]
        copy(ref, ref, d_send, d_recv.at[i], other).wait_recv()
        copy(ref, ref, f_send, f_recv, other).start()
        return 0

    lax.fori_loop(1, NZ, pass_docs, 0)
    step_by(3)
    for k in range(5, 8):
        step_ax(k)
    step_by(4)
    for k in range(8):
        af(k, 2).wait_recv()
    took(dg.at[:, 0], f_recv)

    dt[...] = dg[...].reshape(E, ND)
    for j in range(4):
        block = dt[:, pl.ds(128 * j, 128)].astype(F32)
        scale = 1.0 / jnp.sqrt(jnp.sum(block * block, axis=0, keepdims=True) * (1.0 / E) + 1e-06)
        xn[pl.ds(128 * j, 128), :] = (block * scale).T.astype(BF16)

    ss[...] = jnp.zeros_like(ss)

    def unpack(t, _):
        xx, yy = lax.div(t, 4), 2 * lax.rem(t, 4)
        rows = pl.ds(pl.multiple_of(t * FL, FL), FL)
        for h in range(2):
            if h == 0:
                u0, u1 = ca[xx, yy].astype(F32), ca[xx, yy + 1].astype(F32)
            else:
                u0, u1 = cb[yy, xx].astype(F32), cb[yy + 1, xx].astype(F32)
            for g in range(2):
                part = jnp.concatenate([u0[FD * g:FD * g + FD], u1[FD * g:FD * g + FD]], axis=0)
                cols = pl.ds((2 * h + g) * Q, Q)
                ct[rows, cols] = part.astype(BF16)
                ss[:, cols] += jnp.sum((part * part).reshape(FL // 8, 8, Q), axis=0)
        return 0

    lax.fori_loop(0, NL, unpack, 0)

    rr[...] = jnp.zeros_like(rr)
    T = 256

    def scores(n, _):
        cols = pl.ds(pl.multiple_of(n * T, T), T)
        norm = jnp.sqrt(jnp.sum(ss[:, cols], axis=0, keepdims=True) * (1.0 / E) + 1e-06)
        s = jnp.dot(xn[...], ct[:, cols], preferred_element_type=F32)
        k = jnp.exp(s * (1.0 / (E * 0.02 * norm)))
        kk[:, cols] = k
        rr[...] += k[:, 0:128] + k[:, 128:256]
        return 0

    lax.fori_loop(0, NV // T, scores, 0)

    def reduce_leaf(i):
        pbuf[i, l] = jnp.sum(rr[...].T, axis=0, keepdims=True)

        def send(j, _):
            copy(
                pbuf.at[i, l], pbuf.at[i, l], p_send.at[i], p_recv.at[i], (d, lax.rem(l + j, NL))
            ).start()
            return 0

        lax.fori_loop(1, NL, send, 0)
        took(pbuf.at[i, pl.ds(0, NL - 1)], p_recv.at[i])
        u = 1.0 / jnp.sum(pbuf[i], axis=0)
        ub[...] = jnp.broadcast_to(u, (128, ND)).T

    def columns(i):
        def one(n, _):
            cols = pl.ds(pl.multiple_of(n * 128, 128), 128)
            w = kk[:, cols] * ub[...]
            if i == 1:
                ww[:, cols] = w.astype(BF16)
            ybuf[i, y, :, cols] = jnp.sum(jnp.sum(w.reshape(ND // 8, 8, 128), axis=0), axis=0, keepdims=True)
            return 0

        lax.fori_loop(0, NV // 128, one, 0)

    def send_y(i):
        def send(j, _):
            to = (x * NY + lax.rem(y + j, NY), l)
            copy(ybuf.at[i, y], ybuf.at[i, y], y_send.at[i], y_recv.at[i], to).start()
            return 0

        lax.fori_loop(1, NY, send, 0)

    def send_x(i):
        took(ybuf.at[i, pl.ds(0, NY - 1)], y_recv.at[i])
        xbuf[i, x] = jnp.sum(ybuf[i], axis=0)

        def send(j, _):
            to = (lax.rem(x + j, NX) * NY + y, l)
            copy(xbuf.at[i, x], xbuf.at[i, x], x_send.at[i], x_recv.at[i], to).start()
            return 0

        lax.fori_loop(1, NX, send, 0)

    def take_x(i):
        took(xbuf.at[i, pl.ds(0, NX - 1)], x_recv.at[i])
        vv[...] = RATIO / jnp.sum(xbuf[i], axis=0)

    reduce_leaf(0)
    columns(0)
    send_y(0)
    send_x(0)
    take_x(0)

    rr[...] = jnp.zeros_like(rr)

    def rows_of(n, _):
        cols = pl.ds(pl.multiple_of(n * 128, 128), 128)
        rr[...] += kk[:, cols] * vv[:, cols]
        return 0

    lax.fori_loop(0, NV // 128, rows_of, 0)
    reduce_leaf(1)
    columns(1)
    send_y(1)

    def products(h):
        def one(xx, _):
            rows = pl.ds(pl.multiple_of(xx * 192, 192), 192)
            gs[...] = jnp.dot(dt[rows, :], ww[:, 2 * Q * h:2 * Q * (h + 1)], preferred_element_type=F32)
            for yy in range(NY):
                unit = jnp.concatenate(
                    [gs[FD * yy:FD * yy + FD, 0:Q], gs[FD * yy:FD * yy + FD, Q:2 * Q]], axis=0
                ).astype(BF16)
                if h == 0:
                    oa[xx, yy] = unit
                else:
                    ob[yy, xx] = unit
            return 0

        lax.fori_loop(0, NX, one, 0)

    def rb(way, step, m):
        o = (4 - step) if way == 0 else (step - 4)
        return copy(
            ob.at[at_y(o), at_x(XSEQ[m])], rby.at[way, step, m],
            rb_send.at[way, step, m], rb_recv.at[way, step, m], dev(0, 1 if way == 0 else -1),
        )

    def step_rb(s):
        for way in range(2):
            o = (4 - s) if way == 0 else (s - 4)
            for m in range(4):
                ref = ob.at[at_y(o), at_x(XSEQ[m])]
                if s > 1 or (m < 2 if way == 0 else m >= 2):
                    rb(way, s - 1, m).wait_recv()
                    ref[...] = (ref[...].astype(F32) + rby[way, s - 1, m].astype(F32)).astype(BF16)
                if s < 4:
                    rb(way, s, m).start()

    def ra_first(k):
        yy = at_y(YSEQ[k])
        way = k % 2
        return copy(
            oa.at[at_x(2), yy], ra1.at[k], ra1_send.at[k], ra1_recv.at[k], dev(1 if way == 0 else -1, 0)
        )

    def ra_second(k, way):
        o = 1 if way == 0 else -1
        return copy(
            oa.at[at_x(o), at_y(YSEQ[k])], ra2.at[way, k], ra2_send.at[way, k], ra2_recv.at[way, k], dev(o, 0)
        )

    def ra_last(k):
        o = YSEQ[k]
        return copy(oa.at[x, at_y(o)], ray.at[k], ray_send, ray_recv, dev(0, o))

    products(1)
    for m in range(2):
        rb(0, 0, m).start()
        rb(1, 0, m + 2).start()
    products(0)
    KSEQ = (7, 5, 6, 3, 4, 1, 2, 0)
    for k in KSEQ:
        ra_first(k).start()
    for k in KSEQ:
        ra_second(k, 1 - k % 2).start()
    send_x(1)
    step_rb(1)
    for k in KSEQ:
        way = k % 2
        ra_first(k).wait_recv()
        ref = oa.at[at_x(1 if way == 0 else -1), at_y(YSEQ[k])]
        ref[...] = (ref[...].astype(F32) + ra1[k].astype(F32)).astype(BF16)
        ra_second(k, way).start()
    take_x(1)

    def weigh(n, _):
        cols = pl.ds(pl.multiple_of(n * 128, 128), 128)
        ww[:, cols] = (kk[:, cols] * ub[...] * vv[:, cols]).astype(BF16)
        return 0

    lax.fori_loop(0, NV // 128, weigh, 0)

    def recon(t, _):
        rows = pl.ds(pl.multiple_of(t * 2 * FL, 2 * FL), 2 * FL)
        part = lax.dot_general(ct[rows, :], ww[...], (((1,), (1,)), ((), ())), preferred_element_type=F32)
        qq[0, t] = part[0:FL].astype(BF16)
        qq[1, t] = part[FL:2 * FL].astype(BF16)
        return 0

    lax.fori_loop(0, NZ, recon, 0)
    first = copy(qq.at[1 - c], rq, q1_send, q1_recv, other)
    first.start()

    step_rb(2)

    first.wait_recv()

    def add_other(t, _):
        hq[t] = (qq[c, t].astype(F32) + rq[t].astype(F32)).astype(BF16)
        return 0

    lax.fori_loop(0, NZ, add_other, 0)

    def send_recon(i, _):
        zz = lax.rem(z + i, NZ)
        copy(hq.at[zz], sq.at[i], q2_send, q2_recv, dev_leaf(zz, c)).start()
        return 0

    lax.fori_loop(1, NZ, send_recon, 0)

    step_rb(3)
    for k in KSEQ:
        ref = oa.at[x, at_y(YSEQ[k])]
        ra_second(k, 0).wait_recv()
        ra_second(k, 1).wait_recv()
        ref[...] = (ref[...].astype(F32) + ra2[0, k].astype(F32) + ra2[1, k].astype(F32)).astype(BF16)
        if k:
            ra_last(k).start()
    step_rb(4)

    def rbx_copy(m):
        return copy(ob.at[y, at_x(XSEQ[m])], rbx.at[m], rbx_send, rbx_recv, dev(XSEQ[m], 0))

    for m in range(1, 4):
        rbx_copy(m).start()

    took(sq.at[pl.ds(1, NZ - 1)], q2_recv)
    back = hq[z].astype(F32)
    for i in range(1, NZ):
        back = back + sq[i].astype(F32)
    res_ref[...] = (docs_ref[...].astype(F32) - back).astype(BF16)

    v = vv[...] * (1.0 / RATIO)
    took(rbx.at[pl.ds(1, 3)], rbx_recv)
    total = ob[y, x].astype(F32)
    for m in range(1, 4):
        total = total + rbx[m].astype(F32)
    means_ref[:, 2 * Q:3 * Q] = (total[0:FD] * v[:, 2 * Q:3 * Q]).astype(BF16)
    means_ref[:, 3 * Q:4 * Q] = (total[FD:2 * FD] * v[:, 3 * Q:4 * Q]).astype(BF16)

    took(ray.at[pl.ds(1, NY - 1)], ray_recv)
    total = oa[x, y].astype(F32)
    for k in range(1, NY):
        total = total + ray[k].astype(F32)
    means_ref[:, 0:Q] = (total[0:FD] * v[:, 0:Q]).astype(BF16)
    means_ref[:, Q:2 * Q] = (total[FD:2 * FD] * v[:, Q:2 * Q]).astype(BF16)

    took(dg.at[pl.ds(0, NZ - 1), 0], d_send)
    took(dg.at[:, 0], f_send)
    for s in range(4):
        ay(0, s, 0).wait_send()
        if s < 3:
            ay(1, s, 0).wait_send()
        for m in range(4):
            if s < 3 or m < 2:
                by(0, s, m, 0).wait_send()
            if s < 3 or m >= 2:
                by(1, s, m, 0).wait_send()
            if s > 0 or m < 2:
                rb(0, s, m).wait_send()
            if s > 0 or m >= 2:
                rb(1, s, m).wait_send()
    for k in range(8):
        ax(k, 0).wait_send()
        ax(k, 1).wait_send()
        af(k, 0).wait_send()
        ra_first(k).wait_send()
        ra_second(k, 0).wait_send()
        ra_second(k, 1).wait_send()
    for m in range(3):
        bx(m, 0).wait_send()
    for i in range(2):
        took(pbuf.at[i, pl.ds(0, NL - 1)], p_send.at[i])
        took(ybuf.at[i, pl.ds(0, NY - 1)], y_send.at[i])
        took(xbuf.at[i, pl.ds(0, NX - 1)], x_send.at[i])
    first.wait_send()
    took(sq.at[pl.ds(1, NZ - 1)], q2_send)
    took(rbx.at[pl.ds(1, 3)], rbx_send)
    took(ray.at[pl.ds(1, NY - 1)], ray_send)


def body(docs, centroids):
    dma = pltpu.SemaphoreType.DMA
    residual, means = pl.pallas_call(
        kernel,
        out_shape=(jax.ShapeDtypeStruct((FL, ND), BF16), jax.ShapeDtypeStruct((FD, NV), BF16)),
        in_specs=[pl.BlockSpec(memory_space=pltpu.VMEM)] * 2,
        out_specs=(pl.BlockSpec(memory_space=pltpu.VMEM),) * 2,
        scratch_shapes=[
            pltpu.VMEM((NZ, 2, FL, ND), BF16),
            pltpu.VMEM((NX, NY, 2 * FD, Q), BF16),
            pltpu.VMEM((NY, NX, 2 * FD, Q), BF16),
            pltpu.VMEM((E, NV), BF16),
            pltpu.VMEM((ND, E), BF16),
            pltpu.VMEM((E, ND), BF16),
            pltpu.VMEM((ND, NV), F32),
            pltpu.VMEM((ND, NV), BF16),
            pltpu.VMEM((8, NV), F32),
            pltpu.VMEM((ND, 128), F32),
            pltpu.VMEM((ND, 128), F32),
            pltpu.VMEM((2, NL, 1, ND), F32),
            pltpu.VMEM((2, NY, 1, NV), F32),
            pltpu.VMEM((2, NX, 1, NV), F32),
            pltpu.VMEM((192, 2 * Q), F32),
            pltpu.VMEM((NX, NY, 2 * FD, Q), BF16),
            pltpu.VMEM((NY, NX, 2 * FD, Q), BF16),
            pltpu.VMEM((8, 2 * FD, Q), BF16),
            pltpu.VMEM((2, 8, 2 * FD, Q), BF16),
            pltpu.VMEM((8, 2 * FD, Q), BF16),
            pltpu.VMEM((2, 4, 4, 2 * FD, Q), BF16),
            pltpu.VMEM((4, 2 * FD, Q), BF16),
            pltpu.VMEM((2, NZ, FL, ND), BF16),
            pltpu.VMEM((NZ, FL, ND), BF16),
            pltpu.VMEM((NZ, FL, ND), BF16),
            pltpu.VMEM((NZ, FL, ND), BF16),
            pltpu.VMEM((1, NV), F32),
            dma, dma((NZ,)), dma, dma,
            dma((2, 4)), dma((2, 4)), dma((8, 2)), dma((8, 2)), dma((8,)), dma((8,)),
            dma((3,)), dma((3,)), dma((2, 4, 4)), dma((2, 4, 4)),
            dma((2,)), dma((2,)), dma((2,)), dma((2,)), dma((2,)), dma((2,)),
            dma((2, 4, 4)), dma((2, 4, 4)), dma, dma,
            dma((8,)), dma((8,)), dma((2, 8)), dma((2, 8)), dma, dma,
            dma, dma, dma, dma,
        ],
        compiler_params=pltpu.CompilerParams(
            collective_id=0, has_side_effects=True, vmem_limit_bytes=48 * 2**20
        ),
        cost_estimate=pl.CostEstimate(
            flops=6 * ND * NV * E, bytes_accessed=2 * (ND * FL + NV * FD) * 2, transcendentals=ND * NV
        ),
    )(docs.T, centroids.T)
    return residual.T, means.T


def solution(mesh):
    return jax.shard_map(
        body,
        mesh=mesh,
        in_specs=(P("doc", "leaf"), P("leaf", "doc")),
        out_specs=(P("doc", "leaf"), P("leaf", "doc")),
        check_vma=False,
    )
```

```python
import jax
import jax.numpy as jnp
from jax import lax
from jax.experimental import pallas as pl
from jax.experimental.pallas import tpu as pltpu
from jax.sharding import PartitionSpec as P

MESH = pl.DeviceIdType.MESH
F32 = jnp.float32
BF16 = jnp.bfloat16

E = 768
NX, NY, NZ, NL = 4, 8, 8, 16
FD, FL = 24, 48
ND, NV = 512, 2048
QA, QB = 640, 384
COLS = ((0, QA), (QA, QA), (2 * QA, QB), (2 * QA + QB, QB))
RATIO = 0.5

YSEQ = (0, -1, 1, -2, 2, -3, 3, -4)
XSEQ = (0, -1, 1, 2)
HOPS = ((1, 0), (-1, 0), (2, 0), (-2, 0), (1, -2), (-1, 2), (2, -2))
BACK = ((1, 1), (-1, -1), (2, 2), (-2, -2), (1, 3), (-1, -3), (2, 4))


def kernel(
    docs_hbm, cent_hbm, res_ref, means_ref,
    docs_ref, cent_ref, in_sem, dg, ca, cb, ct, xn, dt, kk, ww, ss, rr, ub, pbuf, ybuf, xbuf,
    gs, oa, ob, ra1, ra2, ray, rby, rbx, qq, rq, sq, vv,
    d_send, d_recv, f_send, f_recv,
    ay_send, ay_recv, ax_send, ax_recv, af_send, af_recv,
    bx_send, bx_recv, by_send, by_recv,
    p_send, p_recv, y_send, y_recv, x_send, x_recv,
    rb_send, rb_recv, rbx_send, rbx_recv,
    ra1_send, ra1_recv, ra2_send, ra2_recv, ray_send, ray_recv,
    q1_send, q1_recv, q2_send, q2_recv,
):
    d = lax.axis_index("doc")
    l = lax.axis_index("leaf")
    x, y = lax.div(d, NY), lax.rem(d, NY)
    z, c = lax.div(l, 2), lax.rem(l, 2)

    def at_x(o):
        return lax.rem(x + o + NX, NX)

    def at_y(o):
        return lax.rem(y + o + NY, NY)

    def at_z(o):
        return lax.rem(z + o + NZ, NZ)

    def dev(ox, oy):
        return (at_x(ox) * NY + at_y(oy), l)

    def dev_leaf(zz, cc):
        return (d, zz * 2 + cc)

    other = dev_leaf(z, 1 - c)

    def copy(src, dst, s, r, to):
        return pltpu.make_async_remote_copy(
            src_ref=src, dst_ref=dst, send_sem=s, recv_sem=r, device_id=to, device_id_type=MESH
        )

    def took(ref, sem):
        pltpu.make_async_copy(ref, ref, sem).wait()

    into = (
        pltpu.make_async_copy(cent_hbm, cent_ref, in_sem.at[0]),
        pltpu.make_async_copy(docs_hbm, docs_ref, in_sem.at[1]),
    )
    for one in into:
        one.start()

    barrier = pltpu.get_barrier_semaphore()

    def greet(to):
        pl.semaphore_signal(barrier, inc=1, device_id=to, device_id_type=MESH)

    def greet_leaf(i, _):
        greet((d, lax.rem(l + i, NL)))
        return 0

    def greet_y(i, _):
        greet((x * NY + lax.rem(y + i, NY), l))
        return 0

    def greet_x(i, _):
        greet((lax.rem(x + i, NX) * NY + y, l))
        return 0

    lax.fori_loop(1, NL, greet_leaf, 0)
    lax.fori_loop(1, NY, greet_y, 0)
    lax.fori_loop(1, NX, greet_x, 0)

    for one in into:
        one.wait()
    c32 = cent_ref[...].astype(F32)
    own = [c32[:, at:at + n] for at, n in COLS]
    ca[x, y] = jnp.concatenate(own[0:2], axis=0).astype(BF16)
    cb[y, x] = jnp.concatenate(own[2:4], axis=0).astype(BF16)
    dg[z, c] = docs_ref[...]

    pl.semaphore_wait(barrier, NL - 1 + NY - 1 + NX - 1)

    def ay(i):
        to, o = HOPS[i]
        ref = ca.at[x, at_y(o)]
        return copy(ref, ref, ay_send.at[i], ay_recv.at[i], dev(0, to))

    def ax(k, way, ox=0):
        ref = ca.at[at_x(ox), at_y(YSEQ[k])]
        return copy(ref, ref, ax_send.at[k, way], ax_recv.at[k, way], dev(1 if way == 0 else -1, 0))

    def af(k, ox):
        ref = ca.at[at_x(ox), at_y(YSEQ[k])]
        return copy(ref, ref, af_send.at[k], af_recv.at[k], dev(1 if k % 2 == 0 else -1, 0))

    def bx(i):
        ref = cb.at[y, x]
        return copy(ref, ref, bx_send.at[i], bx_recv.at[i], dev((1, -1, 2)[i], 0))

    def by(way, step, m, o):
        ref = cb.at[at_y(o), at_x(XSEQ[m])]
        return copy(
            ref, ref, by_send.at[way, step, m], by_recv.at[way, step, m], dev(0, 1 if way == 0 else -1)
        )

    def dz(i):
        to, o = HOPS[i]
        ref = dg.at[at_z(o), c]
        return copy(ref, ref, d_send.at[i], d_recv.at[i], dev_leaf(at_z(to), c))

    def pass_docs(o):
        ref = dg.at[at_z(o), c]
        copy(ref, ref, f_send, f_recv, other).start()

    def start_ax(k):
        ax(k, 0).start()
        ax(k, 1).start()

    def start_by(m):
        by(0, 0, m, 0).start()
        by(1, 0, m, 0).start()

    def step_ay(i):
        ay(i).wait_recv()
        if i == 2:
            ay(4).start()
            ay(6).start()
        if i == 3:
            ay(5).start()
        start_ax(i + 1)

    def step_dz(i):
        dz(i).wait_recv()
        if i == 2:
            dz(4).start()
            dz(6).start()
        if i == 3:
            dz(5).start()
        pass_docs(YSEQ[i + 1])

    def step_bx(i):
        bx(i).wait_recv()
        start_by(i + 1)

    def step_by(s, m):
        if s < 4:
            by(0, s - 1, m, -s).wait_recv()
            if s < 3:
                by(0, s, m, -s).start()
        by(1, s - 1, m, s).wait_recv()
        if s < 4:
            by(1, s, m, s).start()

    def step_ax(k):
        ax(k, 0, -1).wait_recv()
        if k % 2 == 0:
            af(k, -1).start()
        ax(k, 1, 1).wait_recv()
        if k % 2 == 1:
            af(k, 1).start()

    for i in range(4):
        ay(i).start()
    for i in range(3):
        bx(i).start()
    start_by(0)
    start_ax(0)
    for i in range(4):
        dz(i).start()
    pass_docs(0)

    step_ay(0)
    step_ay(1)
    step_bx(0)
    step_bx(1)
    step_ay(2)
    step_ay(3)
    step_by(1, 0)
    step_ax(0)
    step_bx(2)
    for i in range(4):
        step_dz(i)
    step_by(1, 1)
    step_by(1, 2)
    step_by(2, 0)
    step_ax(1)
    step_ax(2)
    for i in range(4, 7):
        step_ay(i)
    step_by(1, 3)
    step_by(2, 1)
    step_by(2, 2)
    step_ax(3)
    step_ax(4)
    step_by(3, 0)
    step_by(2, 3)
    for i in range(4, 7):
        step_dz(i)
    step_by(3, 1)
    step_ax(5)
    step_by(3, 2)
    step_ax(6)
    step_by(3, 3)
    step_by(4, 0)
    step_ax(7)
    for m in range(1, 4):
        step_by(4, m)
    for k in range(8):
        af(k, 2).wait_recv()
    took(dg.at[:, 0], f_recv)

    dt[...] = dg[...].reshape(E, ND)
    for j in range(4):
        block = dt[:, pl.ds(128 * j, 128)].astype(F32)
        scale = 1.0 / jnp.sqrt(jnp.sum(block * block, axis=0, keepdims=True) * (1.0 / E) + 1e-06)
        xn[pl.ds(128 * j, 128), :] = (block * scale).T.astype(BF16)

    ss[...] = jnp.zeros_like(ss)

    def unpack(t, _):
        xx, yy = lax.div(t, 4), 2 * lax.rem(t, 4)
        rows = pl.ds(pl.multiple_of(t * FL, FL), FL)
        for h in range(2):
            if h == 0:
                u0, u1 = ca[xx, yy].astype(F32), ca[xx, yy + 1].astype(F32)
            else:
                u0, u1 = cb[yy, xx].astype(F32), cb[yy + 1, xx].astype(F32)
            for g in range(2):
                part = jnp.concatenate([u0[FD * g:FD * g + FD], u1[FD * g:FD * g + FD]], axis=0)
                at, n = COLS[2 * h + g]
                cols = pl.ds(at, n)
                ct[rows, cols] = part.astype(BF16)
                ss[:, cols] += jnp.sum((part * part).reshape(FL // 8, 8, n), axis=0)
        return 0

    lax.fori_loop(0, NL, unpack, 0)

    rr[...] = jnp.zeros_like(rr)
    T = 256

    def scores(n, _):
        cols = pl.ds(pl.multiple_of(n * T, T), T)
        norm = jnp.sqrt(jnp.sum(ss[:, cols], axis=0, keepdims=True) * (1.0 / E) + 1e-06)
        s = jnp.dot(xn[...], ct[:, cols], preferred_element_type=F32)
        k = jnp.exp(s * (1.0 / (E * 0.02 * norm)))
        kk[:, cols] = k
        rr[...] += k[:, 0:128] + k[:, 128:256]
        return 0

    lax.fori_loop(0, NV // T, scores, 0)

    def reduce_leaf(i):
        pbuf[i, l] = jnp.sum(rr[...].T, axis=0, keepdims=True)

        def send(j, _):
            copy(
                pbuf.at[i, l], pbuf.at[i, l], p_send.at[i], p_recv.at[i], (d, lax.rem(l + j, NL))
            ).start()
            return 0

        lax.fori_loop(1, NL, send, 0)
        took(pbuf.at[i, pl.ds(0, NL - 1)], p_recv.at[i])
        u = 1.0 / jnp.sum(pbuf[i], axis=0)
        ub[...] = jnp.broadcast_to(u, (128, ND)).T

    def columns(i):
        def one(n, _):
            cols = pl.ds(pl.multiple_of(n * 128, 128), 128)
            w = kk[:, cols] * ub[...]
            if i == 1:
                ww[:, cols] = w.astype(BF16)
            ybuf[i, y, :, cols] = jnp.sum(jnp.sum(w.reshape(ND // 8, 8, 128), axis=0), axis=0, keepdims=True)
            return 0

        lax.fori_loop(0, NV // 128, one, 0)

    def send_y(i):
        def send(j, _):
            to = (x * NY + lax.rem(y + j, NY), l)
            copy(ybuf.at[i, y], ybuf.at[i, y], y_send.at[i], y_recv.at[i], to).start()
            return 0

        lax.fori_loop(1, NY, send, 0)

    def send_x(i):
        took(ybuf.at[i, pl.ds(0, NY - 1)], y_recv.at[i])
        xbuf[i, x] = jnp.sum(ybuf[i], axis=0)

        def send(j, _):
            to = (lax.rem(x + j, NX) * NY + y, l)
            copy(xbuf.at[i, x], xbuf.at[i, x], x_send.at[i], x_recv.at[i], to).start()
            return 0

        lax.fori_loop(1, NX, send, 0)

    def take_x(i):
        took(xbuf.at[i, pl.ds(0, NX - 1)], x_recv.at[i])
        vv[...] = RATIO / jnp.sum(xbuf[i], axis=0)

    reduce_leaf(0)
    columns(0)
    send_y(0)
    send_x(0)
    take_x(0)

    rr[...] = jnp.zeros_like(rr)

    def rows_of(n, _):
        cols = pl.ds(pl.multiple_of(n * 128, 128), 128)
        rr[...] += kk[:, cols] * vv[:, cols]
        return 0

    lax.fori_loop(0, NV // 128, rows_of, 0)
    reduce_leaf(1)
    columns(1)
    send_y(1)

    def products(h, xx):
        rows = pl.ds(pl.multiple_of(xx * 192, 192), 192)
        (a0, n0), (a1, n1) = COLS[2 * h], COLS[2 * h + 1]
        gs[:, 0:n0 + n1] = jnp.dot(dt[rows, :], ww[:, a0:a1 + n1], preferred_element_type=F32)
        for yy in range(NY):
            r = FD * yy
            unit = jnp.concatenate([gs[r:r + FD, 0:n0], gs[r:r + FD, n0:n0 + n1]], axis=0).astype(BF16)
            if h == 0:
                oa[xx, yy] = unit
            else:
                ob[yy, xx] = unit

    def add(ref, *others):
        total = ref[...].astype(F32)
        for one in others:
            total = total + one.astype(F32)
        ref[...] = total.astype(BF16)

    def rb(way, step, m):
        o = (3 - step) if way == 0 else (step - 4)
        return copy(
            ob.at[at_y(o), at_x(XSEQ[m])], rby.at[way, step, m],
            rb_send.at[way, step, m], rb_recv.at[way, step, m], dev(0, 1 if way == 0 else -1),
        )

    def step_rb(way, s, m):
        rb(way, s - 1, m).wait_recv()
        add(ob.at[at_y((3 - s) if way == 0 else (s - 4)), at_x(XSEQ[m])], rby[way, s - 1, m])
        if s < (3 if way == 0 else 4):
            rb(way, s, m).start()

    def rbx_copy(m):
        return copy(ob.at[y, at_x(XSEQ[m])], rbx.at[m], rbx_send, rbx_recv, dev(XSEQ[m], 0))

    def ra_first(k):
        way = k % 2
        return copy(
            oa.at[at_x(2), at_y(YSEQ[k])], ra1.at[k], ra1_send.at[k], ra1_recv.at[k],
            dev(1 if way == 0 else -1, 0),
        )

    def ra_second(k, way):
        o = 1 if way == 0 else -1
        return copy(
            oa.at[at_x(o), at_y(YSEQ[k])], ra2.at[way, k], ra2_send.at[way, k], ra2_recv.at[way, k], dev(o, 0)
        )

    def ra_last(i):
        to, o = BACK[i]
        return copy(oa.at[x, at_y(o)], ray.at[i], ray_send.at[i], ray_recv.at[i], dev(0, to))

    def step_ra1(k):
        ra_first(k).wait_recv()
        add(oa.at[at_x(1 if k % 2 == 0 else -1), at_y(YSEQ[k])], ra1[k])
        ra_second(k, k % 2).start()

    def step_ra2(k):
        ra_second(k, 0).wait_recv()
        ra_second(k, 1).wait_recv()
        add(oa.at[x, at_y(YSEQ[k])], ra2[0, k], ra2[1, k])

    KSEQ = (7, 5, 6, 3, 4, 1, 2, 0)
    products(0, at_x(2))
    for k in KSEQ:
        ra_first(k).start()
    for o in (2, 1, -1, 0):
        products(1, at_x(o))
    for m in range(4):
        rb(1, 0, m).start()
        rb(0, 0, m).start()
    products(0, at_x(1))
    for k in KSEQ:
        if k % 2 == 1:
            ra_second(k, 0).start()
    products(0, at_x(-1))
    for k in KSEQ:
        if k % 2 == 0:
            ra_second(k, 1).start()
    products(0, x)
    send_x(1)
    for m in range(4):
        step_rb(1, 1, m)
        step_rb(0, 1, m)
    for k in KSEQ:
        step_ra1(k)
    take_x(1)

    H = ND // 2

    def weigh(n, _):
        cols = pl.ds(pl.multiple_of(n * 128, 128), 128)
        ww[:, cols] = (kk[:, cols] * ub[...] * vv[:, cols]).astype(BF16)
        return 0

    def q_first(h):
        return copy(qq.at[h, 1 - c], rq.at[h], q1_send.at[h], q1_recv.at[h], other)

    def recon(h):
        part = lax.dot_general(
            ct[...], ww[h * H:(h + 1) * H, :], (((1,), (1,)), ((), ())), preferred_element_type=F32
        )
        for t in range(NL):
            qq[h, t % 2, t // 2] = part[FL * t:FL * t + FL].astype(BF16)
        q_first(h).start()

    def q_second(h, i):
        to, o = BACK[i]
        return copy(
            qq.at[h, c, at_z(o)], sq.at[h, i], q2_send.at[h, i], q2_recv.at[h, i], dev_leaf(at_z(to), c)
        )

    def step_q1(h):
        q_first(h).wait_recv()
        for o, i in ((4, 6), (3, 4), (-3, 5), (1, 0), (-1, 1), (2, None), (-2, None), (0, None)):
            add(qq.at[h, c, at_z(o)], rq[h, at_z(o)])
            if i is not None:
                q_second(h, i).start()

    def step_q2(h):
        q_second(h, 5).wait_recv()
        add(qq.at[h, c, at_z(-2)], sq[h, 5])
        q_second(h, 3).start()
        q_second(h, 4).wait_recv()
        q_second(h, 6).wait_recv()
        add(qq.at[h, c, at_z(2)], sq[h, 4], sq[h, 6])
        q_second(h, 2).start()

    def last_q(h):
        back = qq[h, c, z].astype(F32)
        for i in range(4):
            q_second(h, i).wait_recv()
            back = back + sq[h, i].astype(F32)
        cols = slice(h * H, (h + 1) * H)
        res_ref[:, cols] = (docs_ref[:, cols].astype(F32) - back).astype(BF16)

    lax.fori_loop(0, NV // 128, weigh, 0)
    recon(0)
    for m in range(4):
        step_rb(1, 2, m)
        step_rb(0, 2, m)
    recon(1)
    step_q1(0)
    step_ra2(7)
    ra_last(6).start()
    step_ra2(5)
    ra_last(5).start()
    step_ra2(6)
    ra_last(4).start()
    step_q1(1)
    for m in range(4):
        step_rb(1, 3, m)
        step_rb(0, 3, m)
    step_ra2(3)
    step_ra2(4)
    step_q2(0)
    ra_last(5).wait_recv()
    add(oa.at[x, at_y(-2)], ray[5])
    ra_last(3).start()
    ra_last(4).wait_recv()
    ra_last(6).wait_recv()
    add(oa.at[x, at_y(2)], ray[4], ray[6])
    ra_last(2).start()
    step_ra2(1)
    ra_last(1).start()
    step_ra2(2)
    ra_last(0).start()
    step_q2(1)
    for m in (3, 1, 2, 0):
        step_rb(1, 4, m)
        if m:
            rbx_copy(m).start()
    step_ra2(0)
    last_q(0)
    last_q(1)

    v = vv[...] * (1.0 / RATIO)

    def write_means(h, total):
        for g in range(2):
            at, n = COLS[2 * h + g]
            means_ref[:, at:at + n] = (total[FD * g:FD * g + FD] * v[:, at:at + n]).astype(BF16)

    took(rbx.at[pl.ds(1, 3)], rbx_recv)
    total = ob[y, x].astype(F32)
    for m in range(1, 4):
        total = total + rbx[m].astype(F32)
    write_means(1, total)
    total = oa[x, y].astype(F32)
    for i in range(4):
        ra_last(i).wait_recv()
        total = total + ray[i].astype(F32)
    write_means(0, total)

    took(dg.at[:, 0], f_send)
    for i in range(7):
        ay(i).wait_send()
        dz(i).wait_send()
        ra_last(i).wait_send()
        for h in range(2):
            q_second(h, i).wait_send()
    for s in range(4):
        for m in range(4):
            for way in range(2):
                if s < 3 or way == 1:
                    by(way, s, m, 0).wait_send()
                    rb(way, s, m).wait_send()
    for k in range(8):
        ax(k, 0).wait_send()
        ax(k, 1).wait_send()
        af(k, 0).wait_send()
        ra_first(k).wait_send()
        ra_second(k, 0).wait_send()
        ra_second(k, 1).wait_send()
    for i in range(3):
        bx(i).wait_send()
    for i in range(2):
        took(pbuf.at[i, pl.ds(0, NL - 1)], p_send.at[i])
        took(ybuf.at[i, pl.ds(0, NY - 1)], y_send.at[i])
        took(xbuf.at[i, pl.ds(0, NX - 1)], x_send.at[i])
        q_first(i).wait_send()
    took(rbx.at[pl.ds(1, 3)], rbx_send)


def body(docs, centroids):
    dma = pltpu.SemaphoreType.DMA
    residual, means = pl.pallas_call(
        kernel,
        out_shape=(jax.ShapeDtypeStruct((FL, ND), BF16), jax.ShapeDtypeStruct((FD, NV), BF16)),
        in_specs=[pl.BlockSpec(memory_space=pl.ANY)] * 2,
        out_specs=(pl.BlockSpec(memory_space=pltpu.VMEM),) * 2,
        scratch_shapes=[
            pltpu.VMEM((FL, ND), BF16),
            pltpu.VMEM((FD, NV), BF16),
            dma((2,)),
            pltpu.VMEM((NZ, 2, FL, ND), BF16),
            pltpu.VMEM((NX, NY, 2 * FD, QA), BF16),
            pltpu.VMEM((NY, NX, 2 * FD, QB), BF16),
            pltpu.VMEM((E, NV), BF16),
            pltpu.VMEM((ND, E), BF16),
            pltpu.VMEM((E, ND), BF16),
            pltpu.VMEM((ND, NV), F32),
            pltpu.VMEM((ND, NV), BF16),
            pltpu.VMEM((8, NV), F32),
            pltpu.VMEM((ND, 128), F32),
            pltpu.VMEM((ND, 128), F32),
            pltpu.VMEM((2, NL, 1, ND), F32),
            pltpu.VMEM((2, NY, 1, NV), F32),
            pltpu.VMEM((2, NX, 1, NV), F32),
            pltpu.VMEM((192, 2 * QA), F32),
            pltpu.VMEM((NX, NY, 2 * FD, QA), BF16),
            pltpu.VMEM((NY, NX, 2 * FD, QB), BF16),
            pltpu.VMEM((8, 2 * FD, QA), BF16),
            pltpu.VMEM((2, 8, 2 * FD, QA), BF16),
            pltpu.VMEM((7, 2 * FD, QA), BF16),
            pltpu.VMEM((2, 4, 4, 2 * FD, QB), BF16),
            pltpu.VMEM((4, 2 * FD, QB), BF16),
            pltpu.VMEM((2, 2, NZ, FL, ND // 2), BF16),
            pltpu.VMEM((2, NZ, FL, ND // 2), BF16),
            pltpu.VMEM((2, 7, FL, ND // 2), BF16),
            pltpu.VMEM((1, NV), F32),
            dma((7,)), dma((7,)), dma, dma,
            dma((7,)), dma((7,)), dma((8, 2)), dma((8, 2)), dma((8,)), dma((8,)),
            dma((3,)), dma((3,)), dma((2, 4, 4)), dma((2, 4, 4)),
            dma((2,)), dma((2,)), dma((2,)), dma((2,)), dma((2,)), dma((2,)),
            dma((2, 4, 4)), dma((2, 4, 4)), dma, dma,
            dma((8,)), dma((8,)), dma((2, 8)), dma((2, 8)), dma((7,)), dma((7,)),
            dma((2,)), dma((2,)), dma((2, 7)), dma((2, 7)),
        ],
        compiler_params=pltpu.CompilerParams(
            collective_id=0, has_side_effects=True, vmem_limit_bytes=48 * 2**20
        ),
        cost_estimate=pl.CostEstimate(
            flops=6 * ND * NV * E, bytes_accessed=2 * (ND * FL + NV * FD) * 2, transcendentals=ND * NV
        ),
    )(docs.T, centroids.T)
    return residual.T, means.T


def solution(mesh):
    return jax.shard_map(
        body,
        mesh=mesh,
        in_specs=(P("doc", "leaf"), P("leaf", "doc")),
        out_specs=(P("doc", "leaf"), P("leaf", "doc")),
        check_vma=False,
    )
```

```python
import jax
import jax.numpy as jnp
from jax import lax
from jax.experimental import pallas as pl
from jax.experimental.pallas import tpu as pltpu
from jax.sharding import PartitionSpec as P

MESH = pl.DeviceIdType.MESH
F32 = jnp.float32
BF16 = jnp.bfloat16

E = 768
NX, NY, NZ, NL, NP = 4, 8, 8, 16, 4
FD, FL = 24, 48
ND, NV = 512, 2048
Q = 512
RATIO = 0.5

HOPS = ((1, 0), (-1, 0), (2, 0), (-2, 0), (1, -2), (-1, 2))
LAST_HOP = ((2, -2), (-2, 2))
BACK = ((1, 1), (-1, -1), (2, 2), (-2, -2), (1, 3), (-1, -3))
LAST_BACK = ((2, 4), (-2, -4))
ORDER = (2, 3, 0, 1)


def kernel(
    docs_ref, cent_ref, res_ref, means_ref,
    own, dg, cg, ct, xn, dt, kk, ww, ss, rr, ub, pbuf, ybuf, xbuf,
    gs, og, rc, ra1, ra2, rf, rt, qq, sq, qf, rp, vv,
    d1_send, d1_recv, d2_send, d2_recv, dz_send, dz_recv,
    cy_send, cy_recv, cw_send, cw_recv, cx_send, cx_recv, cf_send, cf_recv, cc_send, cc_recv,
    p_send, p_recv, y_send, y_recv, x_send, x_recv,
    rk_send, rk_recv, ra1_send, ra1_recv, ra2_send, ra2_recv, tf_send, tf_recv, ty_send, ty_recv,
    q_send, q_recv, qs_send, qd_send, qp_recv,
):
    d = lax.axis_index("doc")
    l = lax.axis_index("leaf")
    x, y = lax.div(d, NY), lax.rem(d, NY)
    z, a = lax.div(l, 2), lax.rem(l, 2)
    p, b = lax.div(y, 2), lax.rem(y, 2)
    odd = lax.rem(a + b, 2)
    aligned = odd == 0
    crossed = odd == 1

    def at_x(o):
        return lax.rem(x + o + NX, NX)

    def at_p(o):
        return lax.rem(p + o + 2 * NP, NP)

    def at_z(o):
        return lax.rem(z + o + NZ, NZ)

    def device(xx, yy, zz, core):
        return (xx * NY + yy, zz * 2 + core)

    to_p = (1 - odd * (1 - b), 3 - 3 * odd * b)
    from_p = (1 - odd * b, 3 - 3 * odd * (1 - b))

    def slot(n):
        if n < 2:
            return at_p(-from_p[n])
        if n == 2:
            return at_p(-from_p[0] - 1)
        return at_p(odd * (1 - from_p[1]))

    other = device(x, y, z, 1 - a)
    pair = y + 1 - 2 * b

    def copy(src, dst, s, r, to):
        return pltpu.make_async_remote_copy(
            src_ref=src, dst_ref=dst, send_sem=s, recv_sem=r, device_id=to, device_id_type=MESH
        )

    def took(ref, sem):
        pltpu.make_async_copy(ref, ref, sem).wait()

    mine_leaf = z * 2 + b
    mine_doc = p * 2 + a

    def leaf_peer(i):
        g = lax.rem(mine_leaf + i, NL)
        return device(x, 2 * p + lax.rem(g, 2), lax.div(g, 2), a)

    def doc_peer(i):
        g = lax.rem(mine_doc + i, NY)
        return device(x, 2 * lax.div(g, 2) + b, z, lax.rem(g, 2))

    def x_peer(i):
        return device(lax.rem(x + i, NX), y, z, a)

    barrier = pltpu.get_barrier_semaphore()

    def greet(to):
        pl.semaphore_signal(barrier, inc=1, device_id=to, device_id_type=MESH)

    def greet_leaf(i, _):
        greet(leaf_peer(i))
        return 0

    def greet_doc(i, _):
        greet(doc_peer(i))
        return 0

    def greet_x(i, _):
        greet(x_peer(i))
        return 0

    lax.fori_loop(1, NL, greet_leaf, 0)
    lax.fori_loop(1, NY, greet_doc, 0)
    lax.fori_loop(1, NX, greet_x, 0)

    @pl.when(crossed)
    def _():
        for w in range(2):
            greet(device(x, 2 * at_p(to_p[w]) + a, z, b))

    c32 = cent_ref[...].astype(F32)
    for h in range(2):
        at = 2 * Q * h
        own[h] = jnp.concatenate([c32[:, at:at + Q], c32[:, at + Q:at + 2 * Q]], axis=0).astype(BF16)

    @pl.when(aligned)
    def _():
        cg[a, x, p] = own[...]
        dg[z, a] = docs_ref[...]

    pl.semaphore_wait(barrier, NL - 1 + NY - 1 + NX - 1 + 2 * odd)

    def d1():
        return copy(docs_ref, dg.at[z, a], d1_send, d1_recv.at[a], device(x, pair, z, b))

    def d2():
        return copy(docs_ref, dg.at[z, a], d2_send, d2_recv, other)

    def dz(i, k):
        to, o = HOPS[i] if i < 6 else LAST_HOP[k]
        ref = dg.at[at_z(o), k]
        return copy(ref, ref, dz_send.at[i, k], dz_recv.at[i, k], device(x, y, at_z(to), a))

    def cy(w, h):
        return copy(
            own.at[h], cg.at[b, x, p, h], cy_send.at[w, h], cy_recv.at[w, h],
            device(x, 2 * at_p(to_p[w]) + a, z, b),
        )

    def cw(w, h):
        ref = cg.at[a, x, slot(w), h]
        to = 2 * at_p(1 if w == 0 else -1) + b
        return copy(ref, ref, cw_send.at[w, h], cw_recv.at[w, h], device(x, to, z, a))

    def cx(n, h, way, o=0):
        ref = cg.at[a, at_x(o), slot(n), h]
        to = at_x(1 if way == 0 else -1)
        return copy(ref, ref, cx_send.at[n, h, way], cx_recv.at[n, h, way], device(to, y, z, a))

    def cf(n, h, o):
        ref = cg.at[a, at_x(o), slot(n), h]
        to = at_x(1 if h == 0 else -1)
        return copy(ref, ref, cf_send.at[n, h], cf_recv.at[n, h], device(to, y, z, a))

    def pass_on(n, h, o):
        ref = cg.at[a, at_x(o), slot(n), h]
        copy(ref, ref, cc_send, cc_recv, other).start()

    def have(n, h):
        cx(n, h, 0).start()
        cx(n, h, 1).start()
        pass_on(n, h, 0)

    def step_y(w, h):
        cy(w, h).wait_recv()
        if w == h:
            cw(w, h).start()
        else:
            @pl.when(crossed)
            def _():
                cw(w, h).start()
        have(w, h)

    def step_w(h):
        ref = cg.at[a, x, slot(2), h]
        took(ref, cw_recv.at[(1 - odd) * h, h])
        have(2, h)

        @pl.when(crossed)
        def _():
            took(cg.at[a, x, slot(3), h], cw_recv.at[1, h])
            have(3, h)

    def step_x(n, h):
        cx(n, h, 0, -1).wait_recv()
        if h == 0:
            cf(n, h, -1).start()
        cx(n, h, 1, 1).wait_recv()
        if h == 1:
            cf(n, h, 1).start()
        pass_on(n, h, -1)
        pass_on(n, h, 1)

    def step_f(n, h):
        cf(n, h, 2).wait_recv()
        pass_on(n, h, 2)

    def step_z(i, k):
        dz(i, k).wait_recv()
        if i == 2:
            dz(4, k).start()
            if k == 0:
                dz(6, k).start()
        if i == 3:
            dz(5, k).start()
            if k == 1:
                dz(6, k).start()

    for h in range(2):
        cy(0, h).start()
        cy(1, h).start()

        @pl.when(aligned)
        def _():
            have(3, h)

        if h == 0:
            d1().start()

            @pl.when(crossed)
            def _():
                d2().start()

    @pl.when(aligned)
    def _():
        d2().wait_recv()

    @pl.when(crossed)
    def _():
        took(dg.at[z, 0], d1_recv.at[0])
        took(dg.at[z, 1], d1_recv.at[1])

    for k in range(2):
        for i in range(4):
            dz(i, k).start()

    step_y(0, 0)
    step_y(1, 0)

    @pl.when(aligned)
    def _():
        step_x(3, 0)

    step_y(0, 1)
    step_y(1, 1)

    @pl.when(aligned)
    def _():
        step_x(3, 1)
        step_f(3, 0)
        step_f(3, 1)

    step_w(0)
    for i in range(4):
        step_z(i, 0)
    step_x(0, 0)
    step_x(1, 0)
    step_w(1)
    step_x(0, 1)
    step_x(1, 1)
    for i in range(4):
        step_z(i, 1)
    step_f(0, 0)
    step_f(1, 0)
    step_x(2, 0)

    @pl.when(crossed)
    def _():
        step_x(3, 0)

    step_f(0, 1)
    step_f(1, 1)
    step_x(2, 1)

    @pl.when(crossed)
    def _():
        step_x(3, 1)

    for k in range(2):
        for i in range(4, 7):
            step_z(i, k)
    for h in range(2):
        step_f(2, h)

        @pl.when(crossed)
        def _():
            step_f(3, h)

    took(cg.at[0], cc_recv)

    dt[...] = dg[...].reshape(E, ND)
    for j in range(4):
        block = dt[:, pl.ds(128 * j, 128)].astype(F32)
        scale = 1.0 / jnp.sqrt(jnp.sum(block * block, axis=0, keepdims=True) * (1.0 / E) + 1e-06)
        xn[pl.ds(128 * j, 128), :] = (block * scale).T.astype(BF16)

    ss[...] = jnp.zeros_like(ss)

    def unpack(t, _):
        xx, pp = lax.div(t, NP), lax.rem(t, NP)
        rows = pl.ds(pl.multiple_of(t * FL, FL), FL)
        for h in range(2):
            u0, u1 = cg[0, xx, pp, h].astype(F32), cg[1, xx, pp, h].astype(F32)
            for g in range(2):
                part = jnp.concatenate([u0[FD * g:FD * g + FD], u1[FD * g:FD * g + FD]], axis=0)
                cols = pl.ds((2 * h + g) * Q, Q)
                ct[rows, cols] = part.astype(BF16)
                ss[:, cols] += jnp.sum((part * part).reshape(FL // 8, 8, Q), axis=0)
        return 0

    lax.fori_loop(0, NX * NP, unpack, 0)

    rr[...] = jnp.zeros_like(rr)
    T = 256

    def scores(n, _):
        cols = pl.ds(pl.multiple_of(n * T, T), T)
        norm = jnp.sqrt(jnp.sum(ss[:, cols], axis=0, keepdims=True) * (1.0 / E) + 1e-06)
        s = jnp.dot(xn[...], ct[:, cols], preferred_element_type=F32)
        k = jnp.exp(s * (1.0 / (E * 0.02 * norm)))
        kk[:, cols] = k
        rr[...] += k[:, 0:128] + k[:, 128:256]
        return 0

    lax.fori_loop(0, NV // T, scores, 0)

    def reduce_leaf(i):
        pbuf[i, mine_leaf] = jnp.sum(rr[...].T, axis=0, keepdims=True)

        def send(j, _):
            ref = pbuf.at[i, mine_leaf]
            copy(ref, ref, p_send.at[i], p_recv.at[i], leaf_peer(j)).start()
            return 0

        lax.fori_loop(1, NL, send, 0)
        took(pbuf.at[i, pl.ds(0, NL - 1)], p_recv.at[i])
        u = 1.0 / jnp.sum(pbuf[i], axis=0)
        ub[...] = jnp.broadcast_to(u, (128, ND)).T

    def columns(i):
        def one(n, _):
            cols = pl.ds(pl.multiple_of(n * 128, 128), 128)
            w = kk[:, cols] * ub[...]
            if i == 1:
                ww[:, cols] = w.astype(BF16)
            total = jnp.sum(jnp.sum(w.reshape(ND // 8, 8, 128), axis=0), axis=0, keepdims=True)
            ybuf[i, mine_doc, :, cols] = total
            return 0

        lax.fori_loop(0, NV // 128, one, 0)

    def send_y(i):
        def send(j, _):
            ref = ybuf.at[i, mine_doc]
            copy(ref, ref, y_send.at[i], y_recv.at[i], doc_peer(j)).start()
            return 0

        lax.fori_loop(1, NY, send, 0)

    def send_x(i):
        took(ybuf.at[i, pl.ds(0, NY - 1)], y_recv.at[i])
        xbuf[i, x] = jnp.sum(ybuf[i], axis=0)

        def send(j, _):
            copy(xbuf.at[i, x], xbuf.at[i, x], x_send.at[i], x_recv.at[i], x_peer(j)).start()
            return 0

        lax.fori_loop(1, NX, send, 0)

    def take_x(i):
        took(xbuf.at[i, pl.ds(0, NX - 1)], x_recv.at[i])
        vv[...] = RATIO / jnp.sum(xbuf[i], axis=0)

    reduce_leaf(0)
    columns(0)
    send_y(0)
    send_x(0)
    take_x(0)

    rr[...] = jnp.zeros_like(rr)

    def rows_of(n, _):
        cols = pl.ds(pl.multiple_of(n * 128, 128), 128)
        rr[...] += kk[:, cols] * vv[:, cols]
        return 0

    lax.fori_loop(0, NV // 128, rows_of, 0)
    reduce_leaf(1)
    columns(1)
    send_y(1)

    XSEQ = (2, 1, -1, 0)

    def products(i):
        xx = at_x(XSEQ[i])
        rows = pl.ds(pl.multiple_of(xx * 192, 192), 192)
        gs[...] = jnp.dot(dt[rows, :], ww[...], preferred_element_type=F32)
        for yy in range(NY):
            r = FD * yy
            for h in range(2):
                at = 2 * Q * h
                unit = jnp.concatenate([gs[r:r + FD, at:at + Q], gs[r:r + FD, at + Q:at + 2 * Q]], axis=0)
                og[yy % 2, xx, yy // 2, h] = unit.astype(BF16)
        across(i).start()

    def across(i):
        xx = at_x(XSEQ[i])
        return copy(og.at[1 - a, xx], rc.at[xx], rk_send.at[i], rk_recv.at[i], other)

    def add(o, n, h, *others):
        ref = og.at[a, at_x(o), slot(n), h]
        total = ref[...].astype(F32) + rc[at_x(o), slot(n), h].astype(F32)
        for one in others:
            total = total + one.astype(F32)
        return ref, total

    def ra_first(n, h):
        to = at_x(1 if h == 0 else -1)
        return copy(
            og.at[a, at_x(2), slot(n), h], ra1.at[n, h], ra1_send.at[n, h], ra1_recv.at[n, h],
            device(to, y, z, a),
        )

    def ra_second(n, h, way):
        to = at_x(1 if way == 0 else -1)
        return copy(
            og.at[a, to, slot(n), h], ra2.at[way, n, h], ra2_send.at[way, n, h], ra2_recv.at[way, n, h],
            device(to, y, z, a),
        )

    def tf(w, n, h):
        to = 2 * at_p(2 * w - 1) + b
        return copy(og.at[a, x, slot(n), h], rf.at[w, h], tf_send.at[n - 2, h], tf_recv.at[w, h], device(x, to, z, a))

    def ty(n, h):
        return copy(
            og.at[a, x, slot(n), h], rt.at[n, h], ty_send.at[n, h], ty_recv.at[n, h],
            device(x, 2 * slot(n) + a, z, b),
        )

    def step_first():
        for n in ORDER:
            for h in range(2):
                ref, total = add(2, n, h)
                ref[...] = total.astype(BF16)
                ra_first(n, h).start()

    def step_plain(way):
        h = 1 - way
        for n in ORDER:
            ref, total = add(1 if way == 0 else -1, n, h)
            ref[...] = total.astype(BF16)
            ra_second(n, h, way).start()

    def step_joined(n, h):
        ra_first(n, h).wait_recv()
        ref, total = add(1 if h == 0 else -1, n, h, ra1[n, h])
        ref[...] = total.astype(BF16)
        ra_second(n, h, h).start()

    def step_home(n, h):
        ra_second(n, h, 0).wait_recv()
        ra_second(n, h, 1).wait_recv()
        ref, total = add(0, n, h, ra2[0, n, h], ra2[1, n, h])
        at = 2 * Q * h
        low = total[0:FD] * (vv[:, at:at + Q] * (1.0 / RATIO))
        high = total[FD:2 * FD] * (vv[:, at + Q:at + 2 * Q] * (1.0 / RATIO))
        total = jnp.concatenate([low, high], axis=0)
        if n < 2:
            if n == h:
                tf(n, 2, h).wait_recv()
            else:
                @pl.when(crossed)
                def _():
                    tf(n, 2, h).wait_recv()
            total = total + rf[n, h].astype(F32)
        ref[...] = total.astype(BF16)
        if n < 2:
            ty(n, h).start()
        if n == 2:
            tf((1 - odd) * h, n, h).start()
        if n == 3:
            @pl.when(crossed)
            def _():
                tf(1, n, h).start()

            @pl.when(aligned)
            def _():
                rt[2, h] = ref[...]

    @pl.when(aligned)
    def _():
        rf[0, 1] = jnp.zeros((2 * FD, Q), BF16)
        rf[1, 0] = jnp.zeros((2 * FD, Q), BF16)

    @pl.when(crossed)
    def _():
        rt[2] = jnp.zeros((2, 2 * FD, Q), BF16)

    H = ND // 2

    def weigh(n, _):
        cols = pl.ds(pl.multiple_of(n * 128, 128), 128)
        ww[:, cols] = (kk[:, cols] * ub[...] * vv[:, cols]).astype(BF16)
        return 0

    def qz(h, i):
        to, o = BACK[i] if i < 6 else LAST_BACK[h]
        return copy(
            qq.at[h, at_z(o)], sq.at[h, i], q_send.at[h, i], q_recv.at[h, i], device(x, y, at_z(to), a)
        )

    def recon(h):
        part = lax.dot_general(
            ct[...], ww[h * H:(h + 1) * H, :], (((1,), (1,)), ((), ())), preferred_element_type=F32
        )
        for t in range(NL):
            qq[h, t // 2, t % 2] = part[FL * t:FL * t + FL].astype(BF16)
        for i in (6, 4, 5, 0, 1):
            qz(h, i).start()

    def step_q(h):
        for w, (o, into, out) in enumerate(((2, 4, 2), (-2, 5, 3))):
            ref = qq.at[h, at_z(o)]
            qz(h, into).wait_recv()
            total = ref[...].astype(F32) + sq[h, into].astype(F32)
            if w == h:
                qz(h, 6).wait_recv()
                total = total + sq[h, 6].astype(F32)
            ref[...] = total.astype(BF16)
            qz(h, out).start()

    def q_same(h):
        return copy(qf.at[h, a], rp.at[h, 1], qs_send.at[h], qp_recv.at[h, 1], device(x, 2 * p + a, z, a))

    def q_diff(h):
        return copy(
            qf.at[h, 1 - a], rp.at[h, odd], qd_send.at[h], qp_recv.at[h, odd], device(x, 2 * p + a, z, 1 - a)
        )

    def step_pair(h):
        total = qq[h, z].astype(F32)
        for i in range(4):
            qz(h, i).wait_recv()
            total = total + sq[h, i].astype(F32)
        qf[h] = total.astype(BF16)

        @pl.when(crossed)
        def _():
            q_same(h).start()

        @pl.when(aligned)
        def _():
            rp[h, 0] = qf[h, a]

        q_diff(h).start()

    def last_q(h):
        took(rp.at[h, 1], qp_recv.at[h, 1])

        @pl.when(crossed)
        def _():
            took(rp.at[h, 0], qp_recv.at[h, 0])

        cols = slice(h * H, (h + 1) * H)
        back = rp[h, 0].astype(F32) + rp[h, 1].astype(F32)
        res_ref[:, cols] = (docs_ref[:, cols].astype(F32) - back).astype(BF16)

    products(0)
    products(1)
    across(0).wait_recv()
    step_first()
    products(2)
    across(1).wait_recv()
    step_plain(0)
    products(3)
    across(2).wait_recv()
    step_plain(1)
    send_x(1)
    for n in ORDER:
        step_joined(n, 0)
        step_joined(n, 1)
    across(3).wait_recv()
    for i in range(4):
        across(i).wait_send()
    take_x(1)
    lax.fori_loop(0, NV // 128, weigh, 0)
    recon(0)
    for h in range(2):
        step_home(2, h)
    recon(1)
    for h in range(2):
        step_home(3, h)
    step_q(0)
    for h in range(2):
        step_home(0, h)
        step_home(1, h)
    step_q(1)
    step_pair(0)
    step_pair(1)

    for h in range(2):
        total = rt[2, h].astype(F32)
        for n in range(2):
            ty(n, h).wait_recv()
            total = total + rt[n, h].astype(F32)
        at = 2 * Q * h
        means_ref[:, at:at + Q] = total[0:FD].astype(BF16)
        means_ref[:, at + Q:at + 2 * Q] = total[FD:2 * FD].astype(BF16)

    last_q(0)
    last_q(1)

    d1().wait_send()

    @pl.when(crossed)
    def _():
        d2().wait_send()
        cw(0, 1).wait_send()
        cw(1, 0).wait_send()
        for h in range(2):
            tf(1, 3, h).wait_send()
            q_same(h).wait_send()

    for h in range(2):
        cw(h, h).wait_send()
        tf(0, 2, h).wait_send()
        q_diff(h).wait_send()
        for i in range(7):
            qz(h, i).wait_send()
            dz(i, h).wait_send()
        for n in range(4):
            if n < 2:
                cy(n, h).wait_send()
                ty(n, h).wait_send()
            cf(n, h, 0).wait_send()
            ra_first(n, h).wait_send()
            for way in range(2):
                cx(n, h, way).wait_send()
                ra_second(n, h, way).wait_send()
    took(cg.at[0], cc_send)
    for i in range(2):
        took(pbuf.at[i, pl.ds(0, NL - 1)], p_send.at[i])
        took(ybuf.at[i, pl.ds(0, NY - 1)], y_send.at[i])
        took(xbuf.at[i, pl.ds(0, NX - 1)], x_send.at[i])


def body(docs, centroids):
    dma = pltpu.SemaphoreType.DMA
    unit = (2 * FD, Q)
    residual, means = pl.pallas_call(
        kernel,
        out_shape=(jax.ShapeDtypeStruct((FL, ND), BF16), jax.ShapeDtypeStruct((FD, NV), BF16)),
        in_specs=[pl.BlockSpec(memory_space=pltpu.VMEM)] * 2,
        out_specs=(pl.BlockSpec(memory_space=pltpu.VMEM),) * 2,
        scratch_shapes=[
            pltpu.VMEM((2, *unit), BF16),
            pltpu.VMEM((NZ, 2, FL, ND), BF16),
            pltpu.VMEM((2, NX, NP, 2, *unit), BF16),
            pltpu.VMEM((E, NV), BF16),
            pltpu.VMEM((ND, E), BF16),
            pltpu.VMEM((E, ND), BF16),
            pltpu.VMEM((ND, NV), F32),
            pltpu.VMEM((ND, NV), BF16),
            pltpu.VMEM((8, NV), F32),
            pltpu.VMEM((ND, 128), F32),
            pltpu.VMEM((ND, 128), F32),
            pltpu.VMEM((2, NL, 1, ND), F32),
            pltpu.VMEM((2, NY, 1, NV), F32),
            pltpu.VMEM((2, NX, 1, NV), F32),
            pltpu.VMEM((192, NV), F32),
            pltpu.VMEM((2, NX, NP, 2, *unit), BF16),
            pltpu.VMEM((NX, NP, 2, *unit), BF16),
            pltpu.VMEM((NP, 2, *unit), BF16),
            pltpu.VMEM((2, NP, 2, *unit), BF16),
            pltpu.VMEM((2, 2, *unit), BF16),
            pltpu.VMEM((3, 2, *unit), BF16),
            pltpu.VMEM((2, NZ, 2, FL, ND // 2), BF16),
            pltpu.VMEM((2, 7, 2, FL, ND // 2), BF16),
            pltpu.VMEM((2, 2, FL, ND // 2), BF16),
            pltpu.VMEM((2, 2, FL, ND // 2), BF16),
            pltpu.VMEM((1, NV), F32),
            dma, dma((2,)), dma, dma, dma((7, 2)), dma((7, 2)),
            dma((2, 2)), dma((2, 2)), dma((2, 2)), dma((2, 2)), dma((NP, 2, 2)), dma((NP, 2, 2)), dma((NP, 2)), dma((NP, 2)), dma, dma,
            dma((2,)), dma((2,)), dma((2,)), dma((2,)), dma((2,)), dma((2,)),
            dma((4,)), dma((4,)), dma((NP, 2)), dma((NP, 2)), dma((2, NP, 2)), dma((2, NP, 2)),
            dma((2, 2)), dma((2, 2)), dma((2, 2)), dma((2, 2)),
            dma((2, 7)), dma((2, 7)), dma((2,)), dma((2,)), dma((2, 2)),
        ],
        compiler_params=pltpu.CompilerParams(
            collective_id=0, has_side_effects=True, vmem_limit_bytes=48 * 2**20
        ),
        cost_estimate=pl.CostEstimate(
            flops=6 * ND * NV * E, bytes_accessed=2 * (ND * FL + NV * FD) * 2, transcendentals=ND * NV
        ),
    )(docs.T, centroids.T)
    return residual.T, means.T


def solution(mesh):
    return jax.shard_map(
        body,
        mesh=mesh,
        in_specs=(P("doc", "leaf"), P("leaf", "doc")),
        out_specs=(P("doc", "leaf"), P("leaf", "doc")),
        check_vma=False,
    )
```

```python
import jax
import jax.numpy as jnp
from jax import lax
from jax.experimental import pallas as pl
from jax.experimental.pallas import tpu as pltpu
from jax.sharding import PartitionSpec as P

MESH = pl.DeviceIdType.MESH
F32 = jnp.float32
BF16 = jnp.bfloat16

E = 768
NX, NY, NZ, NL, NP = 4, 8, 8, 16, 4
FD, FL = 24, 48
ND, NV = 512, 2048
Q = 512
QA, QB = 384, 256
LATE = 4 * QA
RATIO = 0.5

HOPS = ((1, 0), (-1, 0), (2, 0), (-2, 0), (1, -2), (-1, 2))
LAST_HOP = ((2, -2), (-2, 2))
BACK = ((1, 3), (-1, -3))
LAST_BACK = ((2, 4), (-2, -4))
ORDER = (2, 3, 0, 1)


def kernel(
    docs_ref, cent_ref, res_ref, means_ref,
    own, gb, dg, cg, cgb, ct, xn, dt, kk, ww, ss, rr, ub, pbuf, ybuf, xbuf,
    gs, og, rc, ra1, ra2, rf, rt, qq, sq, rp, vv,
    d1_send, d1_recv, d2_send, d2_recv, dz_send, dz_recv,
    bx_send, bx_recv, by_send, by_recv, bw_send, bw_recv, bc_send, bc_recv,
    cy_send, cy_recv, cw_send, cw_recv, cx_send, cx_recv, cf_send, cf_recv, cc_send, cc_recv,
    p_send, p_recv, y_send, y_recv, x_send, x_recv,
    rk_send, rk_recv, ra1_send, ra1_recv, ra2_send, ra2_recv, tf_send, tf_recv, ty_send, ty_recv,
    q_send, q_recv, qh_send, qh_recv,
):
    d = lax.axis_index("doc")
    l = lax.axis_index("leaf")
    x, y = lax.div(d, NY), lax.rem(d, NY)
    z, a = lax.div(l, 2), lax.rem(l, 2)
    p, b = lax.div(y, 2), lax.rem(y, 2)
    odd = lax.rem(a + b, 2)
    aligned = odd == 0
    crossed = odd == 1

    def at_x(o):
        return lax.rem(x + o + NX, NX)

    def at_p(o):
        return lax.rem(p + o + 2 * NP, NP)

    def at_z(o):
        return lax.rem(z + o + NZ, NZ)

    def device(xx, yy, zz, core):
        return (xx * NY + yy, zz * 2 + core)

    to_p = (1 - odd * (1 - b), 3 - 3 * odd * b)
    from_p = (1 - odd * b, 3 - 3 * odd * (1 - b))

    def slot(n):
        if n < 2:
            return at_p(-from_p[n])
        if n == 2:
            return at_p(-from_p[0] - 1)
        return at_p(odd * (1 - from_p[1]))

    other = device(x, y, z, 1 - a)
    pair = y + 1 - 2 * b

    def copy(src, dst, s, r, to):
        return pltpu.make_async_remote_copy(
            src_ref=src, dst_ref=dst, send_sem=s, recv_sem=r, device_id=to, device_id_type=MESH
        )

    def took(ref, sem):
        pltpu.make_async_copy(ref, ref, sem).wait()

    mine_leaf = z * 2 + b
    mine_doc = p * 2 + a

    def leaf_peer(i):
        g = lax.rem(mine_leaf + i, NL)
        return device(x, 2 * p + lax.rem(g, 2), lax.div(g, 2), a)

    def doc_peer(i):
        g = lax.rem(mine_doc + i, NY)
        return device(x, 2 * lax.div(g, 2) + b, z, lax.rem(g, 2))

    def x_peer(i):
        return device(lax.rem(x + i, NX), y, z, a)

    barrier = pltpu.get_barrier_semaphore()

    def greet(to):
        pl.semaphore_signal(barrier, inc=1, device_id=to, device_id_type=MESH)

    def greet_leaf(i, _):
        greet(leaf_peer(i))
        return 0

    def greet_doc(i, _):
        greet(doc_peer(i))
        return 0

    def greet_x(i, _):
        greet(x_peer(i))
        return 0

    lax.fori_loop(1, NL, greet_leaf, 0)
    lax.fori_loop(1, NY, greet_doc, 0)
    lax.fori_loop(1, NX, greet_x, 0)

    @pl.when(crossed)
    def _():
        for w in range(2):
            greet(device(x, 2 * at_p(to_p[w]) + a, z, b))
        for o in (1, -1, 2, -2):
            greet(device(x, pair, at_z(o), 1 - a))

    for o in (1, -1, 2, -2):
        greet(device(x, y, at_z(o), 1 - a))

    c32 = cent_ref[...].astype(F32)
    for h in range(2):
        at = 2 * QA * h
        own[h] = jnp.concatenate([c32[:, at:at + QA], c32[:, at + QA:at + 2 * QA]], axis=0).astype(BF16)
    gb[x] = jnp.concatenate([c32[:, LATE:LATE + QB], c32[:, LATE + QB:]], axis=0).astype(BF16)

    @pl.when(aligned)
    def _():
        cg[a, x, p] = own[...]
        dg[z, a] = docs_ref[...]

    pl.semaphore_wait(barrier, NL - 1 + NY - 1 + NX - 1 + 4 + 6 * odd)

    def d1():
        return copy(docs_ref, dg.at[z, a], d1_send, d1_recv.at[a], device(x, pair, z, b))

    def d2():
        return copy(docs_ref, dg.at[z, a], d2_send, d2_recv, other)

    def dz(i, k):
        to, o = HOPS[i] if i < 6 else LAST_HOP[k]
        ref = dg.at[at_z(o), k]
        return copy(ref, ref, dz_send.at[i, k], dz_recv.at[i, k], device(x, y, at_z(to), a))

    def cy(w, h):
        return copy(
            own.at[h], cg.at[b, x, p, h], cy_send.at[w, h], cy_recv.at[w, h],
            device(x, 2 * at_p(to_p[w]) + a, z, b),
        )

    def cw(w, h):
        ref = cg.at[a, x, slot(w), h]
        to = 2 * at_p(1 if w == 0 else -1) + b
        return copy(ref, ref, cw_send.at[w, h], cw_recv.at[w, h], device(x, to, z, a))

    def cx(n, h, way, o=0):
        ref = cg.at[a, at_x(o), slot(n), h]
        to = at_x(1 if way == 0 else -1)
        return copy(ref, ref, cx_send.at[n, h, way], cx_recv.at[n, h, way], device(to, y, z, a))

    def cf(n, h, o):
        ref = cg.at[a, at_x(o), slot(n), h]
        to = at_x(2 if n >= 2 else 1 if h == 0 else -1)
        return copy(ref, ref, cf_send.at[n, h], cf_recv.at[n, h], device(to, y, z, a))

    def pass_on(n, h, o):
        ref = cg.at[a, at_x(o), slot(n), h]
        copy(ref, ref, cc_send, cc_recv, other).start()

    def bx(i):
        to = at_x((1, -1, 2)[i])
        return copy(gb.at[x], gb.at[x], bx_send.at[i], bx_recv.at[i], device(to, y, z, a))

    def by(w, h):
        half = pl.ds(2 * h, 2)
        return copy(
            gb.at[half], cgb.at[b, p, half], by_send.at[w, h], by_recv.at[w, h],
            device(x, 2 * at_p(to_p[w]) + a, z, b),
        )

    def bw(w, h):
        ref = cgb.at[a, slot(w), pl.ds(2 * h, 2)]
        to = 2 * at_p(1 if w == 0 else -1) + b
        return copy(ref, ref, bw_send.at[w, h], bw_recv.at[w, h], device(x, to, z, a))

    def pass_b(n, h):
        ref = cgb.at[a, slot(n), pl.ds(2 * h, 2)]
        copy(ref, ref, bc_send, bc_recv, other).start()

    def step_bx():
        for i in range(3):
            bx(i).wait_recv()
        for h in range(2):
            by(0, h).start()
            by(1, h).start()

        @pl.when(aligned)
        def _():
            cgb[a, p] = gb[...]
            pass_b(3, 0)
            pass_b(3, 1)

    def step_by(w, h):
        by(w, h).wait_recv()
        if w == h:
            bw(w, h).start()
        else:
            @pl.when(crossed)
            def _():
                bw(w, h).start()
        pass_b(w, h)

    def step_bw(h):
        half = pl.ds(2 * h, 2)
        took(cgb.at[a, slot(2), half], bw_recv.at[(1 - odd) * h, h])
        pass_b(2, h)

        @pl.when(crossed)
        def _():
            took(cgb.at[a, slot(3), half], bw_recv.at[1, h])
            pass_b(3, h)

    def have(n, h):
        cx(n, h, 0).start()
        cx(n, h, 1).start()
        if n >= 2:
            cf(n, h, 0).start()
        pass_on(n, h, 0)

    def step_y(w, h):
        cy(w, h).wait_recv()
        if w == h:
            cw(w, h).start()
        else:
            @pl.when(crossed)
            def _():
                cw(w, h).start()
        have(w, h)

    def step_w(h):
        ref = cg.at[a, x, slot(2), h]
        took(ref, cw_recv.at[(1 - odd) * h, h])
        have(2, h)

        @pl.when(crossed)
        def _():
            took(cg.at[a, x, slot(3), h], cw_recv.at[1, h])
            have(3, h)

    def step_x(n, h):
        cx(n, h, 0, -1).wait_recv()
        if h == 0 and n < 2:
            cf(n, h, -1).start()
        cx(n, h, 1, 1).wait_recv()
        if h == 1 and n < 2:
            cf(n, h, 1).start()
        pass_on(n, h, -1)
        pass_on(n, h, 1)

    def step_f(n, h):
        cf(n, h, 2).wait_recv()
        pass_on(n, h, 2)

    def step_z(i, k):
        dz(i, k).wait_recv()
        if i == 2:
            dz(4, k).start()
            if k == 0:
                dz(6, k).start()
        if i == 3:
            dz(5, k).start()
            if k == 1:
                dz(6, k).start()

    for h in range(2):
        cy(0, h).start()
        cy(1, h).start()
        if h == 0:
            for i in range(3):
                bx(i).start()

        @pl.when(aligned)
        def _():
            have(3, h)

        if h == 0:
            d1().start()

            @pl.when(crossed)
            def _():
                d2().start()

    @pl.when(aligned)
    def _():
        d2().wait_recv()

    @pl.when(crossed)
    def _():
        took(dg.at[z, 0], d1_recv.at[0])
        took(dg.at[z, 1], d1_recv.at[1])

    for k in range(2):
        for i in range(4):
            dz(i, k).start()

    step_y(0, 0)
    step_y(1, 0)

    @pl.when(aligned)
    def _():
        step_x(3, 0)

    step_y(0, 1)
    step_y(1, 1)
    step_bx()

    @pl.when(aligned)
    def _():
        step_x(3, 1)
        step_f(3, 0)
        step_f(3, 1)

    step_w(0)
    for i in range(4):
        step_z(i, 0)
    step_x(0, 0)
    step_x(1, 0)
    step_w(1)
    for h in range(2):
        step_by(0, h)
        step_by(1, h)
    step_x(0, 1)
    step_x(1, 1)
    for i in range(4):
        step_z(i, 1)
    step_f(0, 0)
    step_f(1, 0)
    step_x(2, 0)

    @pl.when(crossed)
    def _():
        step_x(3, 0)

    step_bw(0)
    step_f(0, 1)
    step_f(1, 1)
    step_x(2, 1)

    @pl.when(crossed)
    def _():
        step_x(3, 1)

    for k in range(2):
        for i in range(4, 7):
            step_z(i, k)
    for h in range(2):
        step_f(2, h)

        @pl.when(crossed)
        def _():
            step_f(3, h)

    step_bw(1)
    took(cg.at[0], cc_recv)
    took(cgb.at[0], bc_recv)

    dt[...] = dg[...].reshape(E, ND)
    for j in range(4):
        block = dt[:, pl.ds(128 * j, 128)].astype(F32)
        scale = 1.0 / jnp.sqrt(jnp.sum(block * block, axis=0, keepdims=True) * (1.0 / E) + 1e-06)
        xn[pl.ds(128 * j, 128), :] = (block * scale).T.astype(BF16)

    ss[...] = jnp.zeros_like(ss)

    def unpack(t, _):
        xx, pp = lax.div(t, NP), lax.rem(t, NP)
        rows = pl.ds(pl.multiple_of(t * FL, FL), FL)
        for h in range(3):
            if h < 2:
                u0, u1, n = cg[0, xx, pp, h].astype(F32), cg[1, xx, pp, h].astype(F32), QA
            else:
                u0, u1, n = cgb[0, pp, xx].astype(F32), cgb[1, pp, xx].astype(F32), QB
            for g in range(2):
                part = jnp.concatenate([u0[FD * g:FD * g + FD], u1[FD * g:FD * g + FD]], axis=0)
                cols = pl.ds(2 * QA * h + n * g, n)
                ct[rows, cols] = part.astype(BF16)
                ss[:, cols] += jnp.sum((part * part).reshape(FL // 8, 8, n), axis=0)
        return 0

    lax.fori_loop(0, NX * NP, unpack, 0)

    rr[...] = jnp.zeros_like(rr)
    T = 256

    def scores(n, _):
        cols = pl.ds(pl.multiple_of(n * T, T), T)
        norm = jnp.sqrt(jnp.sum(ss[:, cols], axis=0, keepdims=True) * (1.0 / E) + 1e-06)
        s = jnp.dot(xn[...], ct[:, cols], preferred_element_type=F32)
        k = jnp.exp(s * (1.0 / (E * 0.02 * norm)))
        kk[:, cols] = k
        rr[...] += k[:, 0:128] + k[:, 128:256]
        return 0

    lax.fori_loop(0, NV // T, scores, 0)

    def reduce_leaf(i):
        pbuf[i, mine_leaf] = jnp.sum(rr[...].T, axis=0, keepdims=True)

        def send(j, _):
            ref = pbuf.at[i, mine_leaf]
            copy(ref, ref, p_send.at[i], p_recv.at[i], leaf_peer(j)).start()
            return 0

        lax.fori_loop(1, NL, send, 0)
        took(pbuf.at[i, pl.ds(0, NL - 1)], p_recv.at[i])
        u = 1.0 / jnp.sum(pbuf[i], axis=0)
        ub[...] = jnp.broadcast_to(u, (128, ND)).T

    def columns(i):
        def one(n, _):
            cols = pl.ds(pl.multiple_of(n * 128, 128), 128)
            w = kk[:, cols] * ub[...]
            if i == 1:
                ww[:, cols] = w.astype(BF16)
            total = jnp.sum(jnp.sum(w.reshape(ND // 8, 8, 128), axis=0), axis=0, keepdims=True)
            xbuf[i, x, :, cols] = total
            return 0

        lax.fori_loop(0, NV // 128, one, 0)

    def send_x(i):
        def send(j, _):
            copy(xbuf.at[i, x], xbuf.at[i, x], x_send.at[i], x_recv.at[i], x_peer(j)).start()
            return 0

        lax.fori_loop(1, NX, send, 0)

    def send_y(i):
        took(xbuf.at[i, pl.ds(0, NX - 1)], x_recv.at[i])
        ybuf[i, mine_doc] = jnp.sum(xbuf[i], axis=0)

        def send(j, _):
            ref = ybuf.at[i, mine_doc]
            copy(ref, ref, y_send.at[i], y_recv.at[i], doc_peer(j)).start()
            return 0

        lax.fori_loop(1, NY, send, 0)

    def take_y(i):
        took(ybuf.at[i, pl.ds(0, NY - 1)], y_recv.at[i])
        vv[...] = RATIO / jnp.sum(ybuf[i], axis=0)

    reduce_leaf(0)
    columns(0)
    send_x(0)
    send_y(0)
    take_y(0)

    rr[...] = jnp.zeros_like(rr)

    def rows_of(n, _):
        cols = pl.ds(pl.multiple_of(n * 128, 128), 128)
        rr[...] += kk[:, cols] * vv[:, cols]
        return 0

    lax.fori_loop(0, NV // 128, rows_of, 0)
    reduce_leaf(1)
    columns(1)
    send_x(1)

    XSEQ = (2, 1, -1, 0)

    def products(i):
        xx = at_x(XSEQ[i])
        rows = pl.ds(pl.multiple_of(xx * 192, 192), 192)
        gs[...] = jnp.dot(dt[rows, :], ww[...], preferred_element_type=F32)
        for yy in range(NY):
            r = FD * yy
            for h in range(2):
                at = 2 * Q * h
                unit = jnp.concatenate([gs[r:r + FD, at:at + Q], gs[r:r + FD, at + Q:at + 2 * Q]], axis=0)
                og[yy % 2, xx, yy // 2, h] = unit.astype(BF16)
        across(i).start()

    def across(i):
        xx = at_x(XSEQ[i])
        return copy(og.at[1 - a, xx], rc.at[xx], rk_send.at[i], rk_recv.at[i], other)

    def add(o, n, h, *others):
        ref = og.at[a, at_x(o), slot(n), h]
        total = ref[...].astype(F32) + rc[at_x(o), slot(n), h].astype(F32)
        for one in others:
            total = total + one.astype(F32)
        return ref, total

    def ra_first(n, h):
        to = at_x(1 if h == 0 else -1)
        return copy(
            og.at[a, at_x(2), slot(n), h], ra1.at[n, h], ra1_send.at[n, h], ra1_recv.at[n, h],
            device(to, y, z, a),
        )

    def ra_second(n, h, way):
        to = at_x(1 if way == 0 else -1)
        return copy(
            og.at[a, to, slot(n), h], ra2.at[way, n, h], ra2_send.at[way, n, h], ra2_recv.at[way, n, h],
            device(to, y, z, a),
        )

    def tf(w, n, h):
        to = 2 * at_p(2 * w - 1) + b
        return copy(og.at[a, x, slot(n), h], rf.at[w, h], tf_send.at[n - 2, h], tf_recv.at[w, h], device(x, to, z, a))

    def ty(n, h):
        return copy(
            og.at[a, x, slot(n), h], rt.at[n, h], ty_send.at[n, h], ty_recv.at[n, h],
            device(x, 2 * slot(n) + a, z, b),
        )

    def step_first():
        for n in ORDER:
            for h in range(2):
                ref, total = add(2, n, h)
                ref[...] = total.astype(BF16)
                ra_first(n, h).start()

    def step_plain(way):
        for n in ORDER:
            for h in range(2):
                if h != way:
                    ref, total = add(1 if way == 0 else -1, n, h)
                    ref[...] = total.astype(BF16)
                    ra_second(n, h, way).start()

    def step_joined(n, h):
        ra_first(n, h).wait_recv()
        ref, total = add(1 if h == 0 else -1, n, h, ra1[n, h])
        ref[...] = total.astype(BF16)
        ra_second(n, h, h).start()

    def step_home(n, h):
        ra_second(n, h, 0).wait_recv()
        ra_second(n, h, 1).wait_recv()
        ref, total = add(0, n, h, ra2[0, n, h], ra2[1, n, h])
        at = 2 * Q * h
        low = total[0:FD] * (vv[:, at:at + Q] * (1.0 / RATIO))
        high = total[FD:2 * FD] * (vv[:, at + Q:at + 2 * Q] * (1.0 / RATIO))
        total = jnp.concatenate([low, high], axis=0)
        if n < 2:
            if n == h:
                tf(n, 2, h).wait_recv()
            else:
                @pl.when(crossed)
                def _():
                    tf(n, 2, h).wait_recv()
            total = total + rf[n, h].astype(F32)
        ref[...] = total.astype(BF16)
        if n < 2:
            ty(n, h).start()
        if n == 2:
            tf((1 - odd) * h, n, h).start()
        if n == 3:
            @pl.when(crossed)
            def _():
                tf(1, n, h).start()

            @pl.when(aligned)
            def _():
                rt[2, h] = ref[...]

    @pl.when(aligned)
    def _():
        rf[0, 1] = jnp.zeros((2 * FD, Q), BF16)
        rf[1, 0] = jnp.zeros((2 * FD, Q), BF16)

    @pl.when(crossed)
    def _():
        rt[2] = jnp.zeros((2, 2 * FD, Q), BF16)

    H = ND // 2

    def weigh(n, _):
        cols = pl.ds(pl.multiple_of(n * 128, 128), 128)
        ww[:, cols] = (kk[:, cols] * ub[...] * vv[:, cols]).astype(BF16)
        return 0

    def qz(h, i):
        to, o = BACK[i] if i < 2 else LAST_BACK[h]
        return copy(
            qq.at[h, at_z(o)], sq.at[h, i], q_send.at[h, i], q_recv.at[h, i], device(x, y, at_z(to), a)
        )

    def q_home(h, o, e):
        to = device(x, 2 * p + a, at_z(o), e)
        copy(qq.at[h, at_z(o), e], rp.at[h, 2 * (o + 2) + b], qh_send.at[h], qh_recv.at[h], to).start()

    def send_home(h, o):
        q_home(h, o, 1 - a)
        if o:
            q_home(h, o, a)
        else:
            @pl.when(crossed)
            def _():
                q_home(h, o, a)

            @pl.when(aligned)
            def _():
                rp[h, 2 * (o + 2) + b] = qq[h, z, a]

    def recon(h):
        part = lax.dot_general(
            ct[...], ww[h * H:(h + 1) * H, :], (((1,), (1,)), ((), ())), preferred_element_type=F32
        )
        for t in range(NL):
            qq[h, t // 2, t % 2] = part[FL * t:FL * t + FL].astype(BF16)
        for i in (2, 0, 1):
            qz(h, i).start()
        for o in (1, -1, 0):
            send_home(h, o)

    def step_q(h):
        for w, o in enumerate((2, -2)):
            ref = qq.at[h, at_z(o)]
            qz(h, w).wait_recv()
            total = ref[...].astype(F32) + sq[h, w].astype(F32)
            if w == h:
                qz(h, 2).wait_recv()
                total = total + sq[h, 2].astype(F32)
            ref[...] = total.astype(BF16)
            send_home(h, o)

    def wait_home(h, sem):
        @pl.when(crossed)
        def _():
            took(rp.at[h], sem.at[h])

        @pl.when(aligned)
        def _():
            took(rp.at[h, pl.ds(0, 9)], sem.at[h])

    def last_q(h):
        wait_home(h, qh_recv)
        cols = slice(h * H, (h + 1) * H)
        back = rp[h, 0].astype(F32)
        for i in range(1, 10):
            back = back + rp[h, i].astype(F32)
        res_ref[:, cols] = (docs_ref[:, cols].astype(F32) - back).astype(BF16)

    products(0)
    products(1)
    across(0).wait_recv()
    step_first()
    products(2)
    send_y(1)
    across(1).wait_recv()
    step_plain(0)
    products(3)
    across(2).wait_recv()
    step_plain(1)
    for n in ORDER:
        step_joined(n, 0)
        step_joined(n, 1)
    across(3).wait_recv()
    for i in range(4):
        across(i).wait_send()
    take_y(1)
    lax.fori_loop(0, NV // 128, weigh, 0)
    recon(0)
    for h in range(2):
        step_home(2, h)
    recon(1)
    for h in range(2):
        step_home(3, h)
    step_q(0)
    step_home(0, 0)
    step_home(1, 0)
    step_q(1)
    step_home(0, 1)
    step_home(1, 1)

    for h in range(2):
        total = rt[2, h].astype(F32)
        for n in range(2):
            ty(n, h).wait_recv()
            total = total + rt[n, h].astype(F32)
        at = 2 * Q * h
        means_ref[:, at:at + Q] = total[0:FD].astype(BF16)
        means_ref[:, at + Q:at + 2 * Q] = total[FD:2 * FD].astype(BF16)

    last_q(0)
    last_q(1)

    d1().wait_send()

    @pl.when(crossed)
    def _():
        d2().wait_send()
        cw(0, 1).wait_send()
        cw(1, 0).wait_send()
        bw(0, 1).wait_send()
        bw(1, 0).wait_send()
        for h in range(2):
            tf(1, 3, h).wait_send()

    for h in range(2):
        cw(h, h).wait_send()
        bw(h, h).wait_send()
        tf(0, 2, h).wait_send()
        wait_home(h, qh_send)
        for i in range(7):
            if i < 3:
                qz(h, i).wait_send()
            dz(i, h).wait_send()
        for n in range(4):
            if n < 2:
                cy(n, h).wait_send()
                by(n, h).wait_send()
                ty(n, h).wait_send()
            cf(n, h, 0).wait_send()
            ra_first(n, h).wait_send()
            for way in range(2):
                cx(n, h, way).wait_send()
                ra_second(n, h, way).wait_send()
    for i in range(3):
        bx(i).wait_send()
    took(cg.at[0], cc_send)
    took(cgb.at[0], bc_send)
    for i in range(2):
        took(pbuf.at[i, pl.ds(0, NL - 1)], p_send.at[i])
        took(ybuf.at[i, pl.ds(0, NY - 1)], y_send.at[i])
        took(xbuf.at[i, pl.ds(0, NX - 1)], x_send.at[i])


def body(docs, centroids):
    dma = pltpu.SemaphoreType.DMA
    unit = (2 * FD, Q)
    residual, means = pl.pallas_call(
        kernel,
        out_shape=(jax.ShapeDtypeStruct((FL, ND), BF16), jax.ShapeDtypeStruct((FD, NV), BF16)),
        in_specs=[pl.BlockSpec(memory_space=pltpu.VMEM)] * 2,
        out_specs=(pl.BlockSpec(memory_space=pltpu.VMEM),) * 2,
        scratch_shapes=[
            pltpu.VMEM((2, 2 * FD, QA), BF16),
            pltpu.VMEM((NX, 2 * FD, QB), BF16),
            pltpu.VMEM((NZ, 2, FL, ND), BF16),
            pltpu.VMEM((2, NX, NP, 2, 2 * FD, QA), BF16),
            pltpu.VMEM((2, NP, NX, 2 * FD, QB), BF16),
            pltpu.VMEM((E, NV), BF16),
            pltpu.VMEM((ND, E), BF16),
            pltpu.VMEM((E, ND), BF16),
            pltpu.VMEM((ND, NV), F32),
            pltpu.VMEM((ND, NV), BF16),
            pltpu.VMEM((8, NV), F32),
            pltpu.VMEM((ND, 128), F32),
            pltpu.VMEM((ND, 128), F32),
            pltpu.VMEM((2, NL, 1, ND), F32),
            pltpu.VMEM((2, NY, 1, NV), F32),
            pltpu.VMEM((2, NX, 1, NV), F32),
            pltpu.VMEM((192, NV), F32),
            pltpu.VMEM((2, NX, NP, 2, *unit), BF16),
            pltpu.VMEM((NX, NP, 2, *unit), BF16),
            pltpu.VMEM((NP, 2, *unit), BF16),
            pltpu.VMEM((2, NP, 2, *unit), BF16),
            pltpu.VMEM((2, 2, *unit), BF16),
            pltpu.VMEM((3, 2, *unit), BF16),
            pltpu.VMEM((2, NZ, 2, FL, ND // 2), BF16),
            pltpu.VMEM((2, 3, 2, FL, ND // 2), BF16),
            pltpu.VMEM((2, 10, FL, ND // 2), BF16),
            pltpu.VMEM((1, NV), F32),
            dma, dma((2,)), dma, dma, dma((7, 2)), dma((7, 2)),
            dma((3,)), dma((3,)), dma((2, 2)), dma((2, 2)), dma((2, 2)), dma((2, 2)), dma, dma,
            dma((2, 2)), dma((2, 2)), dma((2, 2)), dma((2, 2)), dma((NP, 2, 2)), dma((NP, 2, 2)), dma((NP, 2)), dma((NP, 2)), dma, dma,
            dma((2,)), dma((2,)), dma((2,)), dma((2,)), dma((2,)), dma((2,)),
            dma((4,)), dma((4,)), dma((NP, 2)), dma((NP, 2)), dma((2, NP, 2)), dma((2, NP, 2)),
            dma((2, 2)), dma((2, 2)), dma((2, 2)), dma((2, 2)),
            dma((2, 3)), dma((2, 3)), dma((2,)), dma((2,)),
        ],
        compiler_params=pltpu.CompilerParams(
            collective_id=0, has_side_effects=True, vmem_limit_bytes=48 * 2**20
        ),
        cost_estimate=pl.CostEstimate(
            flops=6 * ND * NV * E, bytes_accessed=2 * (ND * FL + NV * FD) * 2, transcendentals=ND * NV
        ),
    )(docs.T, centroids.T)
    return residual.T, means.T


def solution(mesh):
    return jax.shard_map(
        body,
        mesh=mesh,
        in_specs=(P("doc", "leaf"), P("leaf", "doc")),
        out_specs=(P("doc", "leaf"), P("leaf", "doc")),
        check_vma=False,
    )
```

```python
import jax
import jax.numpy as jnp
from jax import lax
from jax.experimental import pallas as pl
from jax.experimental.pallas import tpu as pltpu
from jax.sharding import PartitionSpec as P

MESH = pl.DeviceIdType.MESH
F32 = jnp.float32
BF16 = jnp.bfloat16

E = 768
NX, NY, NZ, NL, NP = 4, 8, 8, 16, 4
FD, FL = 24, 48
ND, NV = 512, 2048
Q = 512
QA, QB = 384, 256
LATE = 4 * QA
RATIO = 0.5

HOPS = ((1, 0), (-1, 0), (2, 0), (-2, 0), (1, -2), (-1, 2))
LAST_HOP = ((2, -2), (-2, 2))
BACK = ((1, 3), (-1, -3))
LAST_BACK = ((2, 4), (-2, -4))
ORDER = (2, 3, 0, 1)


def kernel(
    docs_ref, cent_ref, res_ref, means_ref,
    own, gb, dg, cg, cgb, ct, xn, dt, kk, ww, ss, rr, ub, pbuf, ybuf, xbuf,
    wt, gs, og, rc, ra1, ra2, rf, rt, qq, sq, rp, vv,
    d1_send, d1_recv, d2_send, d2_recv, dz_send, dz_recv,
    bx_send, bx_recv, by_send, by_recv, bw_send, bw_recv, bc_send, bc_recv,
    cy_send, cy_recv, cw_send, cw_recv, cx_send, cx_recv, cf_send, cf_recv, cc_send, cc_recv,
    p_send, p_recv, y_send, y_recv, x_send, x_recv,
    rk_send, rk_recv, ra1_send, ra1_recv, ra2_send, ra2_recv, tf_send, tf_recv, ty_send, ty_recv,
    q_send, q_recv, qh_send, qh_recv,
):
    d = lax.axis_index("doc")
    l = lax.axis_index("leaf")
    x, y = lax.div(d, NY), lax.rem(d, NY)
    z, a = lax.div(l, 2), lax.rem(l, 2)
    p, b = lax.div(y, 2), lax.rem(y, 2)
    odd = lax.rem(a + b, 2)
    aligned = odd == 0
    crossed = odd == 1

    def at_x(o):
        return lax.rem(x + o + NX, NX)

    def at_p(o):
        return lax.rem(p + o + 2 * NP, NP)

    def at_z(o):
        return lax.rem(z + o + NZ, NZ)

    def device(xx, yy, zz, core):
        return (xx * NY + yy, zz * 2 + core)

    to_p = (1 - odd * (1 - b), 3 - 3 * odd * b)
    from_p = (1 - odd * b, 3 - 3 * odd * (1 - b))

    def slot(n):
        if n < 2:
            return at_p(-from_p[n])
        if n == 2:
            return at_p(-from_p[0] - 1)
        return at_p(odd * (1 - from_p[1]))

    other = device(x, y, z, 1 - a)
    pair = y + 1 - 2 * b

    def copy(src, dst, s, r, to):
        return pltpu.make_async_remote_copy(
            src_ref=src, dst_ref=dst, send_sem=s, recv_sem=r, device_id=to, device_id_type=MESH
        )

    def took(ref, sem):
        pltpu.make_async_copy(ref, ref, sem).wait()

    mine_leaf = z * 2 + b
    mine_doc = p * 2 + a

    def leaf_peer(i):
        g = lax.rem(mine_leaf + i, NL)
        return device(x, 2 * p + lax.rem(g, 2), lax.div(g, 2), a)

    def doc_peer(i):
        g = lax.rem(mine_doc + i, NY)
        return device(x, 2 * lax.div(g, 2) + b, z, lax.rem(g, 2))

    def x_peer(i):
        return device(lax.rem(x + i, NX), y, z, a)

    barrier = pltpu.get_barrier_semaphore()

    def greet(to):
        pl.semaphore_signal(barrier, inc=1, device_id=to, device_id_type=MESH)

    def greet_leaf(i, _):
        greet(leaf_peer(i))
        return 0

    def greet_doc(i, _):
        greet(doc_peer(i))
        return 0

    def greet_x(i, _):
        greet(x_peer(i))
        return 0

    lax.fori_loop(1, NL, greet_leaf, 0)
    lax.fori_loop(1, NY, greet_doc, 0)
    lax.fori_loop(1, NX, greet_x, 0)

    @pl.when(crossed)
    def _():
        for w in range(2):
            greet(device(x, 2 * at_p(to_p[w]) + a, z, b))
        for o in (1, -1, 2, -2):
            greet(device(x, pair, at_z(o), 1 - a))

    for o in (1, -1, 2, -2):
        greet(device(x, y, at_z(o), 1 - a))

    c32 = cent_ref[...].astype(F32)
    for h in range(2):
        at = 2 * QA * h
        own[h] = jnp.concatenate([c32[:, at:at + QA], c32[:, at + QA:at + 2 * QA]], axis=0).astype(BF16)
    gb[x] = jnp.concatenate([c32[:, LATE:LATE + QB], c32[:, LATE + QB:]], axis=0).astype(BF16)

    @pl.when(aligned)
    def _():
        cg[a, x, p] = own[...]
        dg[z, a] = docs_ref[...]

    pl.semaphore_wait(barrier, NL - 1 + NY - 1 + NX - 1 + 4 + 6 * odd)

    def d1():
        return copy(docs_ref, dg.at[z, a], d1_send, d1_recv.at[a], device(x, pair, z, b))

    def d2():
        return copy(docs_ref, dg.at[z, a], d2_send, d2_recv, other)

    def dz(i, k):
        to, o = HOPS[i] if i < 6 else LAST_HOP[k]
        ref = dg.at[at_z(o), k]
        return copy(ref, ref, dz_send.at[i, k], dz_recv.at[i, k], device(x, y, at_z(to), a))

    def cy(w, h):
        return copy(
            own.at[h], cg.at[b, x, p, h], cy_send.at[w, h], cy_recv.at[w, h],
            device(x, 2 * at_p(to_p[w]) + a, z, b),
        )

    def cw(w, h):
        ref = cg.at[a, x, slot(w), h]
        to = 2 * at_p(1 if w == 0 else -1) + b
        return copy(ref, ref, cw_send.at[w, h], cw_recv.at[w, h], device(x, to, z, a))

    def cx(n, h, way, o=0):
        ref = cg.at[a, at_x(o), slot(n), h]
        to = at_x(1 if way == 0 else -1)
        return copy(ref, ref, cx_send.at[n, h, way], cx_recv.at[n, h, way], device(to, y, z, a))

    def cf(n, h, o):
        ref = cg.at[a, at_x(o), slot(n), h]
        to = at_x(2 if n >= 2 else 1 if h == 0 else -1)
        return copy(ref, ref, cf_send.at[n, h], cf_recv.at[n, h], device(to, y, z, a))

    def pass_on(n, h, o):
        ref = cg.at[a, at_x(o), slot(n), h]
        copy(ref, ref, cc_send, cc_recv, other).start()

    def bx(i):
        to = at_x((1, -1, 2)[i])
        return copy(gb.at[x], gb.at[x], bx_send.at[i], bx_recv.at[i], device(to, y, z, a))

    def by(w, h):
        half = pl.ds(2 * h, 2)
        return copy(
            gb.at[half], cgb.at[b, p, half], by_send.at[w, h], by_recv.at[w, h],
            device(x, 2 * at_p(to_p[w]) + a, z, b),
        )

    def bw(w, h):
        ref = cgb.at[a, slot(w), pl.ds(2 * h, 2)]
        to = 2 * at_p(1 if w == 0 else -1) + b
        return copy(ref, ref, bw_send.at[w, h], bw_recv.at[w, h], device(x, to, z, a))

    def pass_b(n, h):
        ref = cgb.at[a, slot(n), pl.ds(2 * h, 2)]
        copy(ref, ref, bc_send, bc_recv, other).start()

    def step_bx():
        for i in range(3):
            bx(i).wait_recv()
        for h in range(2):
            by(0, h).start()
            by(1, h).start()

        @pl.when(aligned)
        def _():
            cgb[a, p] = gb[...]
            pass_b(3, 0)
            pass_b(3, 1)

    def step_by(w, h):
        by(w, h).wait_recv()
        if w == h:
            bw(w, h).start()
        else:
            @pl.when(crossed)
            def _():
                bw(w, h).start()
        pass_b(w, h)

    def step_bw(h):
        half = pl.ds(2 * h, 2)
        took(cgb.at[a, slot(2), half], bw_recv.at[(1 - odd) * h, h])
        pass_b(2, h)

        @pl.when(crossed)
        def _():
            took(cgb.at[a, slot(3), half], bw_recv.at[1, h])
            pass_b(3, h)

    def have(n, h):
        cx(n, h, 0).start()
        cx(n, h, 1).start()
        if n >= 2:
            cf(n, h, 0).start()
        pass_on(n, h, 0)

    def step_y(w, h):
        cy(w, h).wait_recv()
        if w == h:
            cw(w, h).start()
        else:
            @pl.when(crossed)
            def _():
                cw(w, h).start()
        have(w, h)

    def step_w(h):
        ref = cg.at[a, x, slot(2), h]
        took(ref, cw_recv.at[(1 - odd) * h, h])
        have(2, h)

        @pl.when(crossed)
        def _():
            took(cg.at[a, x, slot(3), h], cw_recv.at[1, h])
            have(3, h)

    def step_x(n, h):
        cx(n, h, 0, -1).wait_recv()
        if h == 0 and n < 2:
            cf(n, h, -1).start()
        cx(n, h, 1, 1).wait_recv()
        if h == 1 and n < 2:
            cf(n, h, 1).start()
        pass_on(n, h, -1)
        pass_on(n, h, 1)

    def step_f(n, h):
        cf(n, h, 2).wait_recv()
        pass_on(n, h, 2)

    def step_z(i, k):
        dz(i, k).wait_recv()
        if i == 2:
            dz(4, k).start()
            if k == 0:
                dz(6, k).start()
        if i == 3:
            dz(5, k).start()
            if k == 1:
                dz(6, k).start()

    for h in range(2):
        cy(0, h).start()
        cy(1, h).start()
        if h == 0:
            for i in range(3):
                bx(i).start()

        @pl.when(aligned)
        def _():
            have(3, h)

        if h == 0:
            d1().start()

            @pl.when(crossed)
            def _():
                d2().start()

    @pl.when(aligned)
    def _():
        d2().wait_recv()

    @pl.when(crossed)
    def _():
        took(dg.at[z, 0], d1_recv.at[0])
        took(dg.at[z, 1], d1_recv.at[1])

    for k in range(2):
        for i in range(4):
            dz(i, k).start()

    step_y(0, 0)
    step_y(1, 0)

    @pl.when(aligned)
    def _():
        step_x(3, 0)

    step_y(0, 1)
    step_y(1, 1)
    step_bx()

    @pl.when(aligned)
    def _():
        step_x(3, 1)
        step_f(3, 0)
        step_f(3, 1)

    step_w(0)
    for i in range(4):
        step_z(i, 0)
    step_x(0, 0)
    step_x(1, 0)
    step_w(1)
    for h in range(2):
        step_by(0, h)
        step_by(1, h)
    step_x(0, 1)
    step_x(1, 1)
    for i in range(4):
        step_z(i, 1)
    step_f(0, 0)
    step_f(1, 0)
    step_x(2, 0)

    @pl.when(crossed)
    def _():
        step_x(3, 0)

    step_bw(0)
    step_f(0, 1)
    step_f(1, 1)
    step_x(2, 1)

    @pl.when(crossed)
    def _():
        step_x(3, 1)

    for k in range(2):
        for i in range(4, 7):
            step_z(i, k)
    for h in range(2):
        step_f(2, h)

        @pl.when(crossed)
        def _():
            step_f(3, h)

    step_bw(1)
    dt[...] = dg[...].reshape(E, ND)
    for j in range(4):
        block = dt[:, pl.ds(128 * j, 128)].astype(F32)
        scale = 1.0 / jnp.sqrt(jnp.sum(block * block, axis=0, keepdims=True) * (1.0 / E) + 1e-06)
        xn[pl.ds(128 * j, 128), :] = (block * scale).T.astype(BF16)

    took(cg.at[0], cc_recv)
    took(cgb.at[0], bc_recv)

    ss[...] = jnp.zeros_like(ss)

    def unpack(t, _):
        xx, pp = lax.div(t, NP), lax.rem(t, NP)
        rows = pl.ds(pl.multiple_of(t * FL, FL), FL)
        for h in range(3):
            if h < 2:
                u0, u1, n = cg[0, xx, pp, h].astype(F32), cg[1, xx, pp, h].astype(F32), QA
            else:
                u0, u1, n = cgb[0, pp, xx].astype(F32), cgb[1, pp, xx].astype(F32), QB
            for g in range(2):
                part = jnp.concatenate([u0[FD * g:FD * g + FD], u1[FD * g:FD * g + FD]], axis=0)
                cols = pl.ds(2 * QA * h + n * g, n)
                ct[rows, cols] = part.astype(BF16)
                ss[:, cols] += jnp.sum((part * part).reshape(FL // 8, 8, n), axis=0)
        return 0

    lax.fori_loop(0, NX * NP, unpack, 0)

    rr[...] = jnp.zeros_like(rr)
    T = 256

    def scores(n, _):
        cols = pl.ds(pl.multiple_of(n * T, T), T)
        norm = jnp.sqrt(jnp.sum(ss[:, cols], axis=0, keepdims=True) * (1.0 / E) + 1e-06)
        s = jnp.dot(xn[...], ct[:, cols], preferred_element_type=F32)
        k = jnp.exp(s * (1.0 / (E * 0.02 * norm)))
        kk[:, cols] = k
        rr[...] += k[:, 0:128] + k[:, 128:256]
        return 0

    lax.fori_loop(0, NV // T, scores, 0, unroll=4)

    def reduce_leaf(i):
        pbuf[i, mine_leaf] = jnp.sum(rr[...].T, axis=0, keepdims=True)

        def send(j, _):
            ref = pbuf.at[i, mine_leaf]
            copy(ref, ref, p_send.at[i], p_recv.at[i], leaf_peer(j)).start()
            return 0

        lax.fori_loop(1, NL, send, 0)
        took(pbuf.at[i, pl.ds(0, NL - 1)], p_recv.at[i])
        u = 1.0 / jnp.sum(pbuf[i], axis=0)
        ub[...] = jnp.broadcast_to(u, (128, ND)).T

    def columns(i):
        def one(n, _):
            cols = pl.ds(pl.multiple_of(n * 128, 128), 128)
            w = kk[:, cols] * ub[...]
            if i == 1:
                ww[:, cols] = w.astype(BF16)
            total = jnp.sum(jnp.sum(w.reshape(ND // 8, 8, 128), axis=0), axis=0, keepdims=True)
            xbuf[i, x, :, cols] = total
            return 0

        lax.fori_loop(0, NV // 128, one, 0, unroll=2)

    def send_x(i):
        def send(j, _):
            copy(xbuf.at[i, x], xbuf.at[i, x], x_send.at[i], x_recv.at[i], x_peer(j)).start()
            return 0

        lax.fori_loop(1, NX, send, 0)

    def send_y(i):
        took(xbuf.at[i, pl.ds(0, NX - 1)], x_recv.at[i])
        ybuf[i, mine_doc] = jnp.sum(xbuf[i], axis=0)

        def send(j, _):
            ref = ybuf.at[i, mine_doc]
            copy(ref, ref, y_send.at[i], y_recv.at[i], doc_peer(j)).start()
            return 0

        lax.fori_loop(1, NY, send, 0)

    def take_y(i):
        took(ybuf.at[i, pl.ds(0, NY - 1)], y_recv.at[i])
        vv[...] = RATIO / jnp.sum(ybuf[i], axis=0)

    reduce_leaf(0)
    columns(0)
    send_x(0)
    send_y(0)
    take_y(0)

    rr[...] = jnp.zeros_like(rr)

    def rows_of(n, _):
        cols = pl.ds(pl.multiple_of(n * 128, 128), 128)
        rr[...] += kk[:, cols] * vv[:, cols]
        return 0

    lax.fori_loop(0, NV // 128, rows_of, 0, unroll=4)
    reduce_leaf(1)
    columns(1)
    send_x(1)

    XSEQ = (2, 1, -1, 0)

    def products(i):
        xx = at_x(XSEQ[i])
        rows = pl.ds(pl.multiple_of(xx * 192, 192), 192)
        gs[...] = jnp.dot(dt[rows, :], ww[...], preferred_element_type=F32)
        for yy in range(NY):
            r = FD * yy
            for h in range(2):
                at = 2 * Q * h
                unit = jnp.concatenate([gs[r:r + FD, at:at + Q], gs[r:r + FD, at + Q:at + 2 * Q]], axis=0)
                og[yy % 2, xx, yy // 2, h] = unit.astype(BF16)
        across(i).start()

    def across(i):
        xx = at_x(XSEQ[i])
        return copy(og.at[1 - a, xx], rc.at[xx], rk_send.at[i], rk_recv.at[i], other)

    def add(o, n, h, *others):
        ref = og.at[a, at_x(o), slot(n), h]
        total = ref[...].astype(F32) + rc[at_x(o), slot(n), h].astype(F32)
        for one in others:
            total = total + one.astype(F32)
        return ref, total

    def ra_first(n, h):
        to = at_x(1 if h == 0 else -1)
        return copy(
            og.at[a, at_x(2), slot(n), h], ra1.at[n, h], ra1_send.at[n, h], ra1_recv.at[n, h],
            device(to, y, z, a),
        )

    def ra_second(n, h, way):
        to = at_x(1 if way == 0 else -1)
        return copy(
            og.at[a, to, slot(n), h], ra2.at[way, n, h], ra2_send.at[way, n, h], ra2_recv.at[way, n, h],
            device(to, y, z, a),
        )

    def tf(w, n, h):
        to = 2 * at_p(2 * w - 1) + b
        return copy(og.at[a, x, slot(n), h], rf.at[w, h], tf_send.at[n - 2, h], tf_recv.at[w, h], device(x, to, z, a))

    def ty(n, h):
        return copy(
            og.at[a, x, slot(n), h], rt.at[n, h], ty_send.at[n, h], ty_recv.at[n, h],
            device(x, 2 * slot(n) + a, z, b),
        )

    def step_first():
        for n in ORDER:
            for h in range(2):
                ref, total = add(2, n, h)
                ref[...] = total.astype(BF16)
                ra_first(n, h).start()

    def step_plain(way):
        for n in ORDER:
            for h in range(2):
                if h != way:
                    ref, total = add(1 if way == 0 else -1, n, h)
                    ref[...] = total.astype(BF16)
                    ra_second(n, h, way).start()

    def step_joined(n, h):
        ra_first(n, h).wait_recv()
        ref, total = add(1 if h == 0 else -1, n, h, ra1[n, h])
        ref[...] = total.astype(BF16)
        ra_second(n, h, h).start()

    def step_home(n, h):
        ra_second(n, h, 0).wait_recv()
        ra_second(n, h, 1).wait_recv()
        ref, total = add(0, n, h, ra2[0, n, h], ra2[1, n, h])
        at = 2 * Q * h
        low = total[0:FD] * (vv[:, at:at + Q] * (1.0 / RATIO))
        high = total[FD:2 * FD] * (vv[:, at + Q:at + 2 * Q] * (1.0 / RATIO))
        total = jnp.concatenate([low, high], axis=0)
        if n < 2:
            if n == h:
                tf(n, 2, h).wait_recv()
            else:
                @pl.when(crossed)
                def _():
                    tf(n, 2, h).wait_recv()
            total = total + rf[n, h].astype(F32)
        ref[...] = total.astype(BF16)
        if n < 2:
            ty(n, h).start()
        if n == 2:
            tf((1 - odd) * h, n, h).start()
        if n == 3:
            @pl.when(crossed)
            def _():
                tf(1, n, h).start()

            @pl.when(aligned)
            def _():
                rt[2, h] = ref[...]

    @pl.when(aligned)
    def _():
        rf[0, 1] = jnp.zeros((2 * FD, Q), BF16)
        rf[1, 0] = jnp.zeros((2 * FD, Q), BF16)

    @pl.when(crossed)
    def _():
        rt[2] = jnp.zeros((2, 2 * FD, Q), BF16)

    H = ND // 2

    def turn(n, _):
        at = pl.ds(pl.multiple_of(n * 128, 128), 128)
        wt[at, :] = ww[:, at].T
        return 0

    def weigh(t, _):
        rows = pl.ds(pl.multiple_of(t * FL, FL), FL)
        ct[rows, :] = (ct[rows, :].astype(F32) * vv[...]).astype(BF16)
        return 0

    def qz(h, i):
        to, o = BACK[i] if i < 2 else LAST_BACK[h]
        return copy(
            qq.at[h, at_z(o)], sq.at[h, i], q_send.at[h, i], q_recv.at[h, i], device(x, y, at_z(to), a)
        )

    def q_home(h, o, e):
        to = device(x, 2 * p + a, at_z(o), e)
        copy(qq.at[h, at_z(o), e], rp.at[h, 2 * (o + 2) + b], qh_send.at[h], qh_recv.at[h], to).start()

    def send_home(h, o):
        q_home(h, o, 1 - a)
        if o:
            q_home(h, o, a)
        else:
            @pl.when(crossed)
            def _():
                q_home(h, o, a)

            @pl.when(aligned)
            def _():
                rp[h, 2 * (o + 2) + b] = qq[h, z, a]

    def recon(h):
        part = jnp.dot(ct[...], wt[:, h * H:(h + 1) * H], preferred_element_type=F32)
        for t in range(NL):
            qq[h, t // 2, t % 2] = part[FL * t:FL * t + FL].astype(BF16)
        for i in (2, 0, 1):
            qz(h, i).start()

    def step_q(h):
        for w, o in enumerate((2, -2)):
            ref = qq.at[h, at_z(o)]
            qz(h, w).wait_recv()
            total = ref[...].astype(F32) + sq[h, w].astype(F32)
            if w == h:
                qz(h, 2).wait_recv()
                total = total + sq[h, 2].astype(F32)
            ref[...] = total.astype(BF16)
            send_home(h, o)

    def wait_home(h, sem):
        @pl.when(crossed)
        def _():
            took(rp.at[h], sem.at[h])

        @pl.when(aligned)
        def _():
            took(rp.at[h, pl.ds(0, 9)], sem.at[h])

    def last_q(h):
        wait_home(h, qh_recv)
        cols = slice(h * H, (h + 1) * H)
        back = rp[h, 0].astype(F32)
        for i in range(1, 10):
            back = back + rp[h, i].astype(F32)
        res_ref[:, cols] = (docs_ref[:, cols].astype(F32) - back).astype(BF16)

    products(0)
    products(1)
    across(0).wait_recv()
    step_first()
    products(2)
    send_y(1)
    across(1).wait_recv()
    step_plain(0)
    products(3)
    across(2).wait_recv()
    step_plain(1)
    lax.fori_loop(0, NV // 128, turn, 0, unroll=2)
    for n in ORDER:
        step_joined(n, 0)
        step_joined(n, 1)
    across(3).wait_recv()
    for i in range(4):
        across(i).wait_send()
    take_y(1)
    lax.fori_loop(0, NL, weigh, 0, unroll=2)
    recon(0)
    recon(1)
    for h in range(2):
        for o in (1, -1, 0):
            send_home(h, o)
    for h in range(2):
        step_home(2, h)
    for h in range(2):
        step_home(3, h)
    step_q(0)
    step_q(1)
    step_home(0, 0)
    step_home(1, 0)
    step_home(0, 1)
    step_home(1, 1)

    for h in range(2):
        total = rt[2, h].astype(F32)
        for n in range(2):
            ty(n, h).wait_recv()
            total = total + rt[n, h].astype(F32)
        at = 2 * Q * h
        means_ref[:, at:at + Q] = total[0:FD].astype(BF16)
        means_ref[:, at + Q:at + 2 * Q] = total[FD:2 * FD].astype(BF16)

    last_q(0)
    last_q(1)

    d1().wait_send()

    @pl.when(crossed)
    def _():
        d2().wait_send()
        cw(0, 1).wait_send()
        cw(1, 0).wait_send()
        bw(0, 1).wait_send()
        bw(1, 0).wait_send()
        for h in range(2):
            tf(1, 3, h).wait_send()

    for h in range(2):
        cw(h, h).wait_send()
        bw(h, h).wait_send()
        tf(0, 2, h).wait_send()
        wait_home(h, qh_send)
        for i in range(7):
            if i < 3:
                qz(h, i).wait_send()
            dz(i, h).wait_send()
        for n in range(4):
            if n < 2:
                cy(n, h).wait_send()
                by(n, h).wait_send()
                ty(n, h).wait_send()
            cf(n, h, 0).wait_send()
            ra_first(n, h).wait_send()
            for way in range(2):
                cx(n, h, way).wait_send()
                ra_second(n, h, way).wait_send()
    for i in range(3):
        bx(i).wait_send()
    took(cg.at[0], cc_send)
    took(cgb.at[0], bc_send)
    for i in range(2):
        took(pbuf.at[i, pl.ds(0, NL - 1)], p_send.at[i])
        took(ybuf.at[i, pl.ds(0, NY - 1)], y_send.at[i])
        took(xbuf.at[i, pl.ds(0, NX - 1)], x_send.at[i])


def body(docs, centroids):
    dma = pltpu.SemaphoreType.DMA
    unit = (2 * FD, Q)
    residual, means = pl.pallas_call(
        kernel,
        out_shape=(jax.ShapeDtypeStruct((FL, ND), BF16), jax.ShapeDtypeStruct((FD, NV), BF16)),
        in_specs=[pl.BlockSpec(memory_space=pltpu.VMEM)] * 2,
        out_specs=(pl.BlockSpec(memory_space=pltpu.VMEM),) * 2,
        scratch_shapes=[
            pltpu.VMEM((2, 2 * FD, QA), BF16),
            pltpu.VMEM((NX, 2 * FD, QB), BF16),
            pltpu.VMEM((NZ, 2, FL, ND), BF16),
            pltpu.VMEM((2, NX, NP, 2, 2 * FD, QA), BF16),
            pltpu.VMEM((2, NP, NX, 2 * FD, QB), BF16),
            pltpu.VMEM((E, NV), BF16),
            pltpu.VMEM((ND, E), BF16),
            pltpu.VMEM((E, ND), BF16),
            pltpu.VMEM((ND, NV), F32),
            pltpu.VMEM((ND, NV), BF16),
            pltpu.VMEM((8, NV), F32),
            pltpu.VMEM((ND, 128), F32),
            pltpu.VMEM((ND, 128), F32),
            pltpu.VMEM((2, NL, 1, ND), F32),
            pltpu.VMEM((2, NY, 1, NV), F32),
            pltpu.VMEM((2, NX, 1, NV), F32),
            pltpu.VMEM((NV, ND), BF16),
            pltpu.VMEM((192, NV), F32),
            pltpu.VMEM((2, NX, NP, 2, *unit), BF16),
            pltpu.VMEM((NX, NP, 2, *unit), BF16),
            pltpu.VMEM((NP, 2, *unit), BF16),
            pltpu.VMEM((2, NP, 2, *unit), BF16),
            pltpu.VMEM((2, 2, *unit), BF16),
            pltpu.VMEM((3, 2, *unit), BF16),
            pltpu.VMEM((2, NZ, 2, FL, ND // 2), BF16),
            pltpu.VMEM((2, 3, 2, FL, ND // 2), BF16),
            pltpu.VMEM((2, 10, FL, ND // 2), BF16),
            pltpu.VMEM((1, NV), F32),
            dma, dma((2,)), dma, dma, dma((7, 2)), dma((7, 2)),
            dma((3,)), dma((3,)), dma((2, 2)), dma((2, 2)), dma((2, 2)), dma((2, 2)), dma, dma,
            dma((2, 2)), dma((2, 2)), dma((2, 2)), dma((2, 2)), dma((NP, 2, 2)), dma((NP, 2, 2)), dma((NP, 2)), dma((NP, 2)), dma, dma,
            dma((2,)), dma((2,)), dma((2,)), dma((2,)), dma((2,)), dma((2,)),
            dma((4,)), dma((4,)), dma((NP, 2)), dma((NP, 2)), dma((2, NP, 2)), dma((2, NP, 2)),
            dma((2, 2)), dma((2, 2)), dma((2, 2)), dma((2, 2)),
            dma((2, 3)), dma((2, 3)), dma((2,)), dma((2,)),
        ],
        compiler_params=pltpu.CompilerParams(
            collective_id=0, has_side_effects=True, vmem_limit_bytes=48 * 2**20
        ),
        cost_estimate=pl.CostEstimate(
            flops=6 * ND * NV * E, bytes_accessed=2 * (ND * FL + NV * FD) * 2, transcendentals=ND * NV
        ),
    )(docs.T, centroids.T)
    return residual.T, means.T


def solution(mesh):
    return jax.shard_map(
        body,
        mesh=mesh,
        in_specs=(P("doc", "leaf"), P("leaf", "doc")),
        out_specs=(P("doc", "leaf"), P("leaf", "doc")),
        check_vma=False,
    )
```

```python
import jax
import jax.numpy as jnp
from jax import lax
from jax.experimental import pallas as pl
from jax.experimental.pallas import tpu as pltpu
from jax.sharding import PartitionSpec as P

MESH = pl.DeviceIdType.MESH
F32 = jnp.float32
BF16 = jnp.bfloat16

E = 768
NX, NY, NZ, NL, NP = 4, 8, 8, 16, 4
FD, FL = 24, 48
ND, NV = 512, 2048
Q = 512
QA, QB = 384, 256
LATE = 4 * QA
RATIO = 0.5

HOPS = ((1, 0), (-1, 0), (2, 0), (-2, 0), (1, -2), (-1, 2))
LAST_HOP = ((2, -2), (-2, 2))
BACK = ((1, 3), (-1, -3))
LAST_BACK = ((2, 4), (-2, -4))
ORDER = (2, 3, 0, 1)


def kernel(
    docs_ref, cent_ref, res_ref, means_ref,
    own, gb, dg, cg, cgb, ct, xn, dt, kk, ww, ss, rr, ub, pbuf, ybuf, xbuf,
    wt, cv, gs, og, rc, ra1, ra2, rf, rt, qq, sq, rp, vv,
    d1_send, d1_recv, d2_send, d2_recv, dz_send, dz_recv,
    bx_send, bx_recv, by_send, by_recv, bw_send, bw_recv, bc_send, bc_recv,
    cy_send, cy_recv, cw_send, cw_recv, cx_send, cx_recv, cf_send, cf_recv, cc_send, cc_recv,
    p_send, p_recv, y_send, y_recv, x_send, x_recv,
    rk_send, rk_recv, ra1_send, ra1_recv, ra2_send, ra2_recv, tf_send, tf_recv, ty_send, ty_recv,
    q_send, q_recv, qh_send, qh_recv,
):
    d = lax.axis_index("doc")
    l = lax.axis_index("leaf")
    x, y = lax.div(d, NY), lax.rem(d, NY)
    z, a = lax.div(l, 2), lax.rem(l, 2)
    p, b = lax.div(y, 2), lax.rem(y, 2)
    odd = lax.rem(a + b, 2)
    aligned = odd == 0
    crossed = odd == 1

    def at_x(o):
        return lax.rem(x + o + NX, NX)

    def at_p(o):
        return lax.rem(p + o + 2 * NP, NP)

    def at_z(o):
        return lax.rem(z + o + NZ, NZ)

    def device(xx, yy, zz, core):
        return (xx * NY + yy, zz * 2 + core)

    to_p = (1 - odd * (1 - b), 3 - 3 * odd * b)
    from_p = (1 - odd * b, 3 - 3 * odd * (1 - b))

    def slot(n):
        if n < 2:
            return at_p(-from_p[n])
        if n == 2:
            return at_p(-from_p[0] - 1)
        return at_p(odd * (1 - from_p[1]))

    other = device(x, y, z, 1 - a)
    pair = y + 1 - 2 * b

    def copy(src, dst, s, r, to):
        return pltpu.make_async_remote_copy(
            src_ref=src, dst_ref=dst, send_sem=s, recv_sem=r, device_id=to, device_id_type=MESH
        )

    def took(ref, sem):
        pltpu.make_async_copy(ref, ref, sem).wait()

    mine_leaf = z * 2 + b
    mine_doc = p * 2 + a

    def leaf_peer(i):
        g = lax.rem(mine_leaf + i, NL)
        return device(x, 2 * p + lax.rem(g, 2), lax.div(g, 2), a)

    def doc_peer(i):
        g = lax.rem(mine_doc + i, NY)
        return device(x, 2 * lax.div(g, 2) + b, z, lax.rem(g, 2))

    def x_peer(i):
        return device(lax.rem(x + i, NX), y, z, a)

    barrier = pltpu.get_barrier_semaphore()

    def greet(to):
        pl.semaphore_signal(barrier, inc=1, device_id=to, device_id_type=MESH)

    def greet_leaf(i, _):
        greet(leaf_peer(i))
        return 0

    def greet_doc(i, _):
        greet(doc_peer(i))
        return 0

    def greet_x(i, _):
        greet(x_peer(i))
        return 0

    lax.fori_loop(1, NL, greet_leaf, 0)
    lax.fori_loop(1, NY, greet_doc, 0)
    lax.fori_loop(1, NX, greet_x, 0)

    @pl.when(crossed)
    def _():
        for w in range(2):
            greet(device(x, 2 * at_p(to_p[w]) + a, z, b))
        for o in (1, -1, 2, -2):
            greet(device(x, pair, at_z(o), 1 - a))

    for o in (1, -1, 2, -2):
        greet(device(x, y, at_z(o), 1 - a))

    c32 = cent_ref[...].astype(F32)
    for h in range(2):
        at = 2 * QA * h
        own[h] = jnp.concatenate([c32[:, at:at + QA], c32[:, at + QA:at + 2 * QA]], axis=0).astype(BF16)
    gb[x] = jnp.concatenate([c32[:, LATE:LATE + QB], c32[:, LATE + QB:]], axis=0).astype(BF16)

    @pl.when(aligned)
    def _():
        cg[a, x, p] = own[...]
        dg[z, a] = docs_ref[...]

    pl.semaphore_wait(barrier, NL - 1 + NY - 1 + NX - 1 + 4 + 6 * odd)

    def d1():
        return copy(docs_ref, dg.at[z, a], d1_send, d1_recv.at[a], device(x, pair, z, b))

    def d2():
        return copy(docs_ref, dg.at[z, a], d2_send, d2_recv, other)

    def dz(i, k):
        to, o = HOPS[i] if i < 6 else LAST_HOP[k]
        ref = dg.at[at_z(o), k]
        return copy(ref, ref, dz_send.at[i, k], dz_recv.at[i, k], device(x, y, at_z(to), a))

    def cy(w, h):
        return copy(
            own.at[h], cg.at[b, x, p, h], cy_send.at[w, h], cy_recv.at[w, h],
            device(x, 2 * at_p(to_p[w]) + a, z, b),
        )

    def cw(w, h):
        ref = cg.at[a, x, slot(w), h]
        to = 2 * at_p(1 if w == 0 else -1) + b
        return copy(ref, ref, cw_send.at[w, h], cw_recv.at[w, h], device(x, to, z, a))

    def cx(n, h, way, o=0):
        ref = cg.at[a, at_x(o), slot(n), h]
        to = at_x(1 if way == 0 else -1)
        return copy(ref, ref, cx_send.at[n, h, way], cx_recv.at[n, h, way], device(to, y, z, a))

    def cf(n, h, o):
        ref = cg.at[a, at_x(o), slot(n), h]
        to = at_x(2 if n >= 2 else 1 if h == 0 else -1)
        return copy(ref, ref, cf_send.at[n, h], cf_recv.at[n, h], device(to, y, z, a))

    def pass_on(n, h, o):
        ref = cg.at[a, at_x(o), slot(n), h]
        copy(ref, ref, cc_send, cc_recv, other).start()

    def bx(i):
        to = at_x((1, -1, 2)[i])
        return copy(gb.at[x], gb.at[x], bx_send.at[i], bx_recv.at[i], device(to, y, z, a))

    def by(w, h):
        half = pl.ds(2 * h, 2)
        return copy(
            gb.at[half], cgb.at[b, p, half], by_send.at[w, h], by_recv.at[w, h],
            device(x, 2 * at_p(to_p[w]) + a, z, b),
        )

    def bw(w, h):
        ref = cgb.at[a, slot(w), pl.ds(2 * h, 2)]
        to = 2 * at_p(1 if w == 0 else -1) + b
        return copy(ref, ref, bw_send.at[w, h], bw_recv.at[w, h], device(x, to, z, a))

    def pass_b(n, h):
        ref = cgb.at[a, slot(n), pl.ds(2 * h, 2)]
        copy(ref, ref, bc_send, bc_recv, other).start()

    def step_bx():
        for i in range(3):
            bx(i).wait_recv()
        for h in range(2):
            by(0, h).start()
            by(1, h).start()

        @pl.when(aligned)
        def _():
            cgb[a, p] = gb[...]
            pass_b(3, 0)
            pass_b(3, 1)

    def step_by(w, h):
        by(w, h).wait_recv()
        if w == h:
            bw(w, h).start()
        else:
            @pl.when(crossed)
            def _():
                bw(w, h).start()
        pass_b(w, h)

    def step_bw(h):
        half = pl.ds(2 * h, 2)
        took(cgb.at[a, slot(2), half], bw_recv.at[(1 - odd) * h, h])
        pass_b(2, h)

        @pl.when(crossed)
        def _():
            took(cgb.at[a, slot(3), half], bw_recv.at[1, h])
            pass_b(3, h)

    def have(n, h):
        cx(n, h, 0).start()
        cx(n, h, 1).start()
        if n >= 2:
            cf(n, h, 0).start()
        pass_on(n, h, 0)

    def step_y(w, h):
        cy(w, h).wait_recv()
        if w == h:
            cw(w, h).start()
        else:
            @pl.when(crossed)
            def _():
                cw(w, h).start()
        have(w, h)

    def step_w(h):
        ref = cg.at[a, x, slot(2), h]
        took(ref, cw_recv.at[(1 - odd) * h, h])
        have(2, h)

        @pl.when(crossed)
        def _():
            took(cg.at[a, x, slot(3), h], cw_recv.at[1, h])
            have(3, h)

    def step_x(n, h):
        cx(n, h, 0, -1).wait_recv()
        if h == 0 and n < 2:
            cf(n, h, -1).start()
        cx(n, h, 1, 1).wait_recv()
        if h == 1 and n < 2:
            cf(n, h, 1).start()
        pass_on(n, h, -1)
        pass_on(n, h, 1)

    def step_f(n, h):
        cf(n, h, 2).wait_recv()
        pass_on(n, h, 2)

    def step_z(i, k):
        dz(i, k).wait_recv()
        if i == 2:
            dz(4, k).start()
            if k == 0:
                dz(6, k).start()
        if i == 3:
            dz(5, k).start()
            if k == 1:
                dz(6, k).start()

    for h in range(2):
        cy(0, h).start()
        cy(1, h).start()
        if h == 0:
            for i in range(3):
                bx(i).start()

        @pl.when(aligned)
        def _():
            have(3, h)

        if h == 0:
            d1().start()

            @pl.when(crossed)
            def _():
                d2().start()

    @pl.when(aligned)
    def _():
        d2().wait_recv()

    @pl.when(crossed)
    def _():
        took(dg.at[z, 0], d1_recv.at[0])
        took(dg.at[z, 1], d1_recv.at[1])

    for k in range(2):
        for i in range(4):
            dz(i, k).start()

    step_y(0, 0)
    step_y(1, 0)

    @pl.when(aligned)
    def _():
        step_x(3, 0)

    step_y(0, 1)
    step_y(1, 1)
    step_bx()

    @pl.when(aligned)
    def _():
        step_x(3, 1)
        step_f(3, 0)
        step_f(3, 1)

    step_w(0)
    for i in range(4):
        step_z(i, 0)
    step_x(0, 0)
    step_x(1, 0)
    step_w(1)
    for h in range(2):
        step_by(0, h)
        step_by(1, h)
    step_x(0, 1)
    step_x(1, 1)
    for i in range(4):
        step_z(i, 1)
    step_f(0, 0)
    step_f(1, 0)
    step_x(2, 0)

    @pl.when(crossed)
    def _():
        step_x(3, 0)

    step_bw(0)
    step_f(0, 1)
    step_f(1, 1)
    step_x(2, 1)

    @pl.when(crossed)
    def _():
        step_x(3, 1)

    for k in range(2):
        for i in range(4, 7):
            step_z(i, k)
    for h in range(2):
        step_f(2, h)

        @pl.when(crossed)
        def _():
            step_f(3, h)

    step_bw(1)
    dt[...] = dg[...].reshape(E, ND)
    for j in range(4):
        block = dt[:, pl.ds(128 * j, 128)].astype(F32)
        scale = 1.0 / jnp.sqrt(jnp.sum(block * block, axis=0, keepdims=True) * (1.0 / E) + 1e-06)
        xn[pl.ds(128 * j, 128), :] = (block * scale).T.astype(BF16)

    took(cg.at[0], cc_recv)
    took(cgb.at[0], bc_recv)

    ss[...] = jnp.zeros_like(ss)

    def unpack(t, _):
        xx, pp = lax.div(t, NP), lax.rem(t, NP)
        rows = pl.ds(pl.multiple_of(t * FL, FL), FL)
        for h in range(3):
            if h < 2:
                u0, u1, n = cg[0, xx, pp, h].astype(F32), cg[1, xx, pp, h].astype(F32), QA
            else:
                u0, u1, n = cgb[0, pp, xx].astype(F32), cgb[1, pp, xx].astype(F32), QB
            for g in range(2):
                part = jnp.concatenate([u0[FD * g:FD * g + FD], u1[FD * g:FD * g + FD]], axis=0)
                cols = pl.ds(2 * QA * h + n * g, n)
                ct[rows, cols] = part.astype(BF16)
                ss[:, cols] += jnp.sum((part * part).reshape(FL // 8, 8, n), axis=0)
        return 0

    lax.fori_loop(0, NX * NP, unpack, 0)

    rr[...] = jnp.zeros_like(rr)
    T = 256

    def scores(n, _):
        cols = pl.ds(pl.multiple_of(n * T, T), T)
        norm = jnp.sqrt(jnp.sum(ss[:, cols], axis=0, keepdims=True) * (1.0 / E) + 1e-06)
        s = jnp.dot(xn[...], ct[:, cols], preferred_element_type=F32)
        k = jnp.exp(s * (1.0 / (E * 0.02 * norm)))
        kk[:, cols] = k
        rr[...] += k[:, 0:128] + k[:, 128:256]
        return 0

    lax.fori_loop(0, NV // T, scores, 0, unroll=4)

    def reduce_leaf(i):
        pbuf[i, mine_leaf] = jnp.sum(rr[...].T, axis=0, keepdims=True)

        def send(j, _):
            ref = pbuf.at[i, mine_leaf]
            copy(ref, ref, p_send.at[i], p_recv.at[i], leaf_peer(j)).start()
            return 0

        lax.fori_loop(1, NL, send, 0)
        took(pbuf.at[i, pl.ds(0, NL - 1)], p_recv.at[i])
        u = 1.0 / jnp.sum(pbuf[i], axis=0)
        ub[...] = jnp.broadcast_to(u, (128, ND)).T

    def columns(i):
        def one(n, _):
            cols = pl.ds(pl.multiple_of(n * 128, 128), 128)
            w = kk[:, cols] * ub[...]
            if i == 1:
                ww[:, cols] = w.astype(BF16)
            total = jnp.sum(jnp.sum(w.reshape(ND // 8, 8, 128), axis=0), axis=0, keepdims=True)
            xbuf[i, x, :, cols] = total
            return 0

        lax.fori_loop(0, NV // 128, one, 0, unroll=2)

    def send_x(i):
        def send(j, _):
            copy(xbuf.at[i, x], xbuf.at[i, x], x_send.at[i], x_recv.at[i], x_peer(j)).start()
            return 0

        lax.fori_loop(1, NX, send, 0)

    def send_y(i):
        took(xbuf.at[i, pl.ds(0, NX - 1)], x_recv.at[i])
        ybuf[i, mine_doc] = jnp.sum(xbuf[i], axis=0)

        def send(j, _):
            ref = ybuf.at[i, mine_doc]
            copy(ref, ref, y_send.at[i], y_recv.at[i], doc_peer(j)).start()
            return 0

        lax.fori_loop(1, NY, send, 0)

    def take_y(i):
        took(ybuf.at[i, pl.ds(0, NY - 1)], y_recv.at[i])
        vv[...] = RATIO / jnp.sum(ybuf[i], axis=0)

    reduce_leaf(0)
    columns(0)
    send_x(0)
    send_y(0)
    take_y(0)

    rr[...] = jnp.zeros_like(rr)

    def rows_of(n, _):
        cols = pl.ds(pl.multiple_of(n * 128, 128), 128)
        rr[...] += kk[:, cols] * vv[:, cols]
        return 0

    lax.fori_loop(0, NV // 128, rows_of, 0, unroll=4)
    reduce_leaf(1)
    columns(1)
    send_x(1)

    XSEQ = (2, 1, -1, 0)

    def products(i):
        xx = at_x(XSEQ[i])
        rows = pl.ds(pl.multiple_of(xx * 192, 192), 192)
        gs[...] = jnp.dot(dt[rows, :], ww[...], preferred_element_type=F32)
        for yy in range(NY):
            r = FD * yy
            for h in range(2):
                at = 2 * Q * h
                unit = jnp.concatenate([gs[r:r + FD, at:at + Q], gs[r:r + FD, at + Q:at + 2 * Q]], axis=0)
                og[yy % 2, xx, yy // 2, h] = unit.astype(BF16)
        across(i).start()

    def across(i):
        xx = at_x(XSEQ[i])
        return copy(og.at[1 - a, xx], rc.at[xx], rk_send.at[i], rk_recv.at[i], other)

    def add(o, n, h, *others):
        ref = og.at[a, at_x(o), slot(n), h]
        total = ref[...].astype(F32) + rc[at_x(o), slot(n), h].astype(F32)
        for one in others:
            total = total + one.astype(F32)
        return ref, total

    def ra_first(n, h):
        to = at_x(1 if h == 0 else -1)
        return copy(
            og.at[a, at_x(2), slot(n), h], ra1.at[n, h], ra1_send.at[n, h], ra1_recv.at[n, h],
            device(to, y, z, a),
        )

    def ra_second(n, h, way):
        to = at_x(1 if way == 0 else -1)
        return copy(
            og.at[a, to, slot(n), h], ra2.at[way, n, h], ra2_send.at[way, n, h], ra2_recv.at[way, n, h],
            device(to, y, z, a),
        )

    def tf(w, n, h):
        to = 2 * at_p(2 * w - 1) + b
        return copy(og.at[a, x, slot(n), h], rf.at[w, h], tf_send.at[n - 2, h], tf_recv.at[w, h], device(x, to, z, a))

    def ty(n, h):
        return copy(
            og.at[a, x, slot(n), h], rt.at[n, h], ty_send.at[n, h], ty_recv.at[n, h],
            device(x, 2 * slot(n) + a, z, b),
        )

    def step_first():
        for n in ORDER:
            for h in range(2):
                ref, total = add(2, n, h)
                ref[...] = total.astype(BF16)
                ra_first(n, h).start()

    def step_plain(way):
        for n in ORDER:
            for h in range(2):
                if h != way:
                    ref, total = add(1 if way == 0 else -1, n, h)
                    ref[...] = total.astype(BF16)
                    ra_second(n, h, way).start()

    def step_joined(n, h):
        ra_first(n, h).wait_recv()
        ref, total = add(1 if h == 0 else -1, n, h, ra1[n, h])
        ref[...] = total.astype(BF16)
        ra_second(n, h, h).start()

    def step_home(n, h):
        ra_second(n, h, 0).wait_recv()
        ra_second(n, h, 1).wait_recv()
        ref, total = add(0, n, h, ra2[0, n, h], ra2[1, n, h])
        at = 2 * Q * h
        low = total[0:FD] * (vv[:, at:at + Q] * (1.0 / RATIO))
        high = total[FD:2 * FD] * (vv[:, at + Q:at + 2 * Q] * (1.0 / RATIO))
        total = jnp.concatenate([low, high], axis=0)
        if n < 2:
            if n == h:
                tf(n, 2, h).wait_recv()
            else:
                @pl.when(crossed)
                def _():
                    tf(n, 2, h).wait_recv()
            total = total + rf[n, h].astype(F32)
        ref[...] = total.astype(BF16)
        if n < 2:
            ty(n, h).start()
        if n == 2:
            tf((1 - odd) * h, n, h).start()
        if n == 3:
            @pl.when(crossed)
            def _():
                tf(1, n, h).start()

            @pl.when(aligned)
            def _():
                rt[2, h] = ref[...]

    @pl.when(aligned)
    def _():
        rf[0, 1] = jnp.zeros((2 * FD, Q), BF16)
        rf[1, 0] = jnp.zeros((2 * FD, Q), BF16)

    @pl.when(crossed)
    def _():
        rt[2] = jnp.zeros((2, 2 * FD, Q), BF16)

    H = ND // 2

    def turn(n, _):
        at = pl.ds(pl.multiple_of(n * 128, 128), 128)
        wt[at, :] = ww[:, at].T
        return 0

    def qz(h, i):
        to, o = BACK[i] if i < 2 else LAST_BACK[h]
        return copy(
            qq.at[h, at_z(o)], sq.at[h, i], q_send.at[h, i], q_recv.at[h, i], device(x, y, at_z(to), a)
        )

    def q_home(h, o, e):
        to = device(x, 2 * p + a, at_z(o), e)
        copy(qq.at[h, at_z(o), e], rp.at[h, 2 * (o + 2) + b], qh_send.at[h], qh_recv.at[h], to).start()

    def send_home(h, o):
        q_home(h, o, 1 - a)
        if o:
            q_home(h, o, a)
        else:
            @pl.when(crossed)
            def _():
                q_home(h, o, a)

            @pl.when(aligned)
            def _():
                rp[h, 2 * (o + 2) + b] = qq[h, z, a]

    def recon(targets, at):
        for i, o in enumerate(targets):
            rows = pl.ds(pl.multiple_of(at_z(o) * 2 * FL, 2 * FL), 2 * FL)
            r = at + 2 * FL * i
            cv[r:r + 2 * FL, :] = (ct[rows, :].astype(F32) * vv[...]).astype(BF16)
        part = jnp.dot(cv[at:at + 2 * FL * len(targets), :], wt[...], preferred_element_type=F32)
        for i, o in enumerate(targets):
            for e in range(2):
                r = (2 * i + e) * FL
                for h in range(2):
                    qq[h, at_z(o), e] = part[r:r + FL, h * H:(h + 1) * H].astype(BF16)

    def step_q(h):
        for w, o in enumerate((2, -2)):
            ref = qq.at[h, at_z(o)]
            qz(h, w).wait_recv()
            total = ref[...].astype(F32) + sq[h, w].astype(F32)
            if w == h:
                qz(h, 2).wait_recv()
                total = total + sq[h, 2].astype(F32)
            ref[...] = total.astype(BF16)
            send_home(h, o)

    def wait_home(h, sem):
        @pl.when(crossed)
        def _():
            took(rp.at[h], sem.at[h])

        @pl.when(aligned)
        def _():
            took(rp.at[h, pl.ds(0, 9)], sem.at[h])

    def last_q(h):
        wait_home(h, qh_recv)
        cols = slice(h * H, (h + 1) * H)
        back = rp[h, 0].astype(F32)
        for i in range(1, 10):
            back = back + rp[h, i].astype(F32)
        res_ref[:, cols] = (docs_ref[:, cols].astype(F32) - back).astype(BF16)

    products(0)
    products(1)
    across(0).wait_recv()
    step_first()
    products(2)
    send_y(1)
    across(1).wait_recv()
    step_plain(0)
    products(3)
    across(2).wait_recv()
    step_plain(1)
    lax.fori_loop(0, NV // 128, turn, 0, unroll=2)
    for n in ORDER:
        step_joined(n, 0)
        step_joined(n, 1)
    across(3).wait_recv()
    for i in range(4):
        across(i).wait_send()
    take_y(1)
    recon((4, 3, -3), 0)
    for h in range(2):
        for i in (2, 0, 1):
            qz(h, i).start()
    recon((2, -2, 1, -1, 0), 6 * FL)
    for h in range(2):
        for o in (1, -1, 0):
            send_home(h, o)
    for h in range(2):
        step_home(2, h)
    for h in range(2):
        step_home(3, h)
    step_q(0)
    step_q(1)
    step_home(0, 0)
    step_home(1, 0)
    step_home(0, 1)
    step_home(1, 1)

    for h in range(2):
        total = rt[2, h].astype(F32)
        for n in range(2):
            ty(n, h).wait_recv()
            total = total + rt[n, h].astype(F32)
        at = 2 * Q * h
        means_ref[:, at:at + Q] = total[0:FD].astype(BF16)
        means_ref[:, at + Q:at + 2 * Q] = total[FD:2 * FD].astype(BF16)

    last_q(0)
    last_q(1)

    d1().wait_send()

    @pl.when(crossed)
    def _():
        d2().wait_send()
        cw(0, 1).wait_send()
        cw(1, 0).wait_send()
        bw(0, 1).wait_send()
        bw(1, 0).wait_send()
        for h in range(2):
            tf(1, 3, h).wait_send()

    for h in range(2):
        cw(h, h).wait_send()
        bw(h, h).wait_send()
        tf(0, 2, h).wait_send()
        wait_home(h, qh_send)
        for i in range(7):
            if i < 3:
                qz(h, i).wait_send()
            dz(i, h).wait_send()
        for n in range(4):
            if n < 2:
                cy(n, h).wait_send()
                by(n, h).wait_send()
                ty(n, h).wait_send()
            cf(n, h, 0).wait_send()
            ra_first(n, h).wait_send()
            for way in range(2):
                cx(n, h, way).wait_send()
                ra_second(n, h, way).wait_send()
    for i in range(3):
        bx(i).wait_send()
    took(cg.at[0], cc_send)
    took(cgb.at[0], bc_send)
    for i in range(2):
        took(pbuf.at[i, pl.ds(0, NL - 1)], p_send.at[i])
        took(ybuf.at[i, pl.ds(0, NY - 1)], y_send.at[i])
        took(xbuf.at[i, pl.ds(0, NX - 1)], x_send.at[i])


def body(docs, centroids):
    dma = pltpu.SemaphoreType.DMA
    unit = (2 * FD, Q)
    residual, means = pl.pallas_call(
        kernel,
        out_shape=(jax.ShapeDtypeStruct((FL, ND), BF16), jax.ShapeDtypeStruct((FD, NV), BF16)),
        in_specs=[pl.BlockSpec(memory_space=pltpu.VMEM)] * 2,
        out_specs=(pl.BlockSpec(memory_space=pltpu.VMEM),) * 2,
        scratch_shapes=[
            pltpu.VMEM((2, 2 * FD, QA), BF16),
            pltpu.VMEM((NX, 2 * FD, QB), BF16),
            pltpu.VMEM((NZ, 2, FL, ND), BF16),
            pltpu.VMEM((2, NX, NP, 2, 2 * FD, QA), BF16),
            pltpu.VMEM((2, NP, NX, 2 * FD, QB), BF16),
            pltpu.VMEM((E, NV), BF16),
            pltpu.VMEM((ND, E), BF16),
            pltpu.VMEM((E, ND), BF16),
            pltpu.VMEM((ND, NV), F32),
            pltpu.VMEM((ND, NV), BF16),
            pltpu.VMEM((8, NV), F32),
            pltpu.VMEM((ND, 128), F32),
            pltpu.VMEM((ND, 128), F32),
            pltpu.VMEM((2, NL, 1, ND), F32),
            pltpu.VMEM((2, NY, 1, NV), F32),
            pltpu.VMEM((2, NX, 1, NV), F32),
            pltpu.VMEM((NV, ND), BF16),
            pltpu.VMEM((E, NV), BF16),
            pltpu.VMEM((192, NV), F32),
            pltpu.VMEM((2, NX, NP, 2, *unit), BF16),
            pltpu.VMEM((NX, NP, 2, *unit), BF16),
            pltpu.VMEM((NP, 2, *unit), BF16),
            pltpu.VMEM((2, NP, 2, *unit), BF16),
            pltpu.VMEM((2, 2, *unit), BF16),
            pltpu.VMEM((3, 2, *unit), BF16),
            pltpu.VMEM((2, NZ, 2, FL, ND // 2), BF16),
            pltpu.VMEM((2, 3, 2, FL, ND // 2), BF16),
            pltpu.VMEM((2, 10, FL, ND // 2), BF16),
            pltpu.VMEM((1, NV), F32),
            dma, dma((2,)), dma, dma, dma((7, 2)), dma((7, 2)),
            dma((3,)), dma((3,)), dma((2, 2)), dma((2, 2)), dma((2, 2)), dma((2, 2)), dma, dma,
            dma((2, 2)), dma((2, 2)), dma((2, 2)), dma((2, 2)), dma((NP, 2, 2)), dma((NP, 2, 2)), dma((NP, 2)), dma((NP, 2)), dma, dma,
            dma((2,)), dma((2,)), dma((2,)), dma((2,)), dma((2,)), dma((2,)),
            dma((4,)), dma((4,)), dma((NP, 2)), dma((NP, 2)), dma((2, NP, 2)), dma((2, NP, 2)),
            dma((2, 2)), dma((2, 2)), dma((2, 2)), dma((2, 2)),
            dma((2, 3)), dma((2, 3)), dma((2,)), dma((2,)),
        ],
        compiler_params=pltpu.CompilerParams(
            collective_id=0, has_side_effects=True, vmem_limit_bytes=48 * 2**20
        ),
        cost_estimate=pl.CostEstimate(
            flops=6 * ND * NV * E, bytes_accessed=2 * (ND * FL + NV * FD) * 2, transcendentals=ND * NV
        ),
    )(docs.T, centroids.T)
    return residual.T, means.T


def solution(mesh):
    return jax.shard_map(
        body,
        mesh=mesh,
        in_specs=(P("doc", "leaf"), P("leaf", "doc")),
        out_specs=(P("doc", "leaf"), P("leaf", "doc")),
        check_vma=False,
    )
```

```python
import jax
import jax.numpy as jnp
from jax import lax
from jax.experimental import pallas as pl
from jax.experimental.pallas import tpu as pltpu
from jax.sharding import PartitionSpec as P

MESH = pl.DeviceIdType.MESH
F32 = jnp.float32
BF16 = jnp.bfloat16

E = 768
NX, NY, NZ, NL, NP = 4, 8, 8, 16, 4
FD, FL = 24, 48
ND, NV = 512, 2048
Q = 512
QA, QB = 384, 256
LATE = 4 * QA
RATIO = 0.5

HOPS = ((1, 0), (-1, 0), (2, 0), (-2, 0), (1, -2), (-1, 2))
LAST_HOP = ((2, -2), (-2, 2))
BACK = ((1, 3), (-1, -3))
LAST_BACK = ((2, 4), (-2, -4))
ORDER = (2, 3, 0, 1)


def kernel(
    docs_ref, cent_ref, res_ref, means_ref,
    own, gb, dg, cg, cgb, ct, xn, dt, kk, ww, ss, rr, ub, pbuf, ybuf, xbuf,
    wt, cv, gs, og, rc, ra1, ra2, rf, rt, qq, sq, rp, vv,
    d1_send, d1_recv, d2_send, d2_recv, dz_send, dz_recv,
    bx_send, bx_recv, by_send, by_recv, bw_send, bw_recv, bc_send, bc_recv,
    cy_send, cy_recv, cw_send, cw_recv, cx_send, cx_recv, cf_send, cf_recv, cc_send, cc_recv,
    p_send, p_recv, y_send, y_recv, x_send, x_recv,
    rk_send, rk_recv, ra1_send, ra1_recv, ra2_send, ra2_recv, tf_send, tf_recv, ty_send, ty_recv,
    q_send, q_recv, qh_send, qh_recv,
):
    d = lax.axis_index("doc")
    l = lax.axis_index("leaf")
    x, y = lax.div(d, NY), lax.rem(d, NY)
    z, a = lax.div(l, 2), lax.rem(l, 2)
    p, b = lax.div(y, 2), lax.rem(y, 2)
    odd = lax.rem(a + b, 2)
    aligned = odd == 0
    crossed = odd == 1

    def at_x(o):
        return lax.rem(x + o + NX, NX)

    def at_p(o):
        return lax.rem(p + o + 2 * NP, NP)

    def at_z(o):
        return lax.rem(z + o + NZ, NZ)

    def device(xx, yy, zz, core):
        return (xx * NY + yy, zz * 2 + core)

    to_p = (1 - odd * (1 - b), 3 - 3 * odd * b)
    from_p = (1 - odd * b, 3 - 3 * odd * (1 - b))

    def slot(n):
        if n < 2:
            return at_p(-from_p[n])
        if n == 2:
            return at_p(-from_p[0] - 1)
        return at_p(odd * (1 - from_p[1]))

    other = device(x, y, z, 1 - a)
    pair = y + 1 - 2 * b

    def copy(src, dst, s, r, to):
        return pltpu.make_async_remote_copy(
            src_ref=src, dst_ref=dst, send_sem=s, recv_sem=r, device_id=to, device_id_type=MESH
        )

    def took(ref, sem):
        pltpu.make_async_copy(ref, ref, sem).wait()

    mine_leaf = z * 2 + b
    mine_doc = p * 2 + a

    def leaf_peer(i):
        g = lax.rem(mine_leaf + i, NL)
        return device(x, 2 * p + lax.rem(g, 2), lax.div(g, 2), a)

    def doc_peer(i):
        g = lax.rem(mine_doc + i, NY)
        return device(x, 2 * lax.div(g, 2) + b, z, lax.rem(g, 2))

    def x_peer(i):
        return device(lax.rem(x + i, NX), y, z, a)

    barrier = pltpu.get_barrier_semaphore()

    def greet(to):
        pl.semaphore_signal(barrier, inc=1, device_id=to, device_id_type=MESH)

    def greet_leaf(i, _):
        greet(leaf_peer(i))
        return 0

    def greet_doc(i, _):
        greet(doc_peer(i))
        return 0

    def greet_x(i, _):
        greet(x_peer(i))
        return 0

    lax.fori_loop(1, NL, greet_leaf, 0)
    lax.fori_loop(1, NY, greet_doc, 0)
    lax.fori_loop(1, NX, greet_x, 0)

    @pl.when(crossed)
    def _():
        for w in range(2):
            greet(device(x, 2 * at_p(to_p[w]) + a, z, b))
        for o in (1, -1, 2, -2):
            greet(device(x, pair, at_z(o), 1 - a))

    for o in (1, -1, 2, -2):
        greet(device(x, y, at_z(o), 1 - a))

    c32 = cent_ref[...].astype(F32)
    for h in range(2):
        at = 2 * QA * h
        own[h] = jnp.concatenate([c32[:, at:at + QA], c32[:, at + QA:at + 2 * QA]], axis=0).astype(BF16)
    gb[x] = jnp.concatenate([c32[:, LATE:LATE + QB], c32[:, LATE + QB:]], axis=0).astype(BF16)

    @pl.when(aligned)
    def _():
        cg[a, x, p] = own[...]
        dg[z, a] = docs_ref[...]

    pl.semaphore_wait(barrier, NL - 1 + NY - 1 + NX - 1 + 4 + 6 * odd)

    def d1():
        return copy(docs_ref, dg.at[z, a], d1_send, d1_recv.at[a], device(x, pair, z, b))

    def d2():
        return copy(docs_ref, dg.at[z, a], d2_send, d2_recv, other)

    def dz(i, k):
        to, o = HOPS[i] if i < 6 else LAST_HOP[k]
        ref = dg.at[at_z(o), k]
        return copy(ref, ref, dz_send.at[i, k], dz_recv.at[i, k], device(x, y, at_z(to), a))

    def cy(w, h):
        return copy(
            own.at[h], cg.at[b, x, p, h], cy_send.at[w, h], cy_recv.at[w, h],
            device(x, 2 * at_p(to_p[w]) + a, z, b),
        )

    def cw(w, h):
        ref = cg.at[a, x, slot(w), h]
        to = 2 * at_p(1 if w == 0 else -1) + b
        return copy(ref, ref, cw_send.at[w, h], cw_recv.at[w, h], device(x, to, z, a))

    def cx(n, h, way, o=0):
        ref = cg.at[a, at_x(o), slot(n), h]
        to = at_x(1 if way == 0 else -1)
        return copy(ref, ref, cx_send.at[n, h, way], cx_recv.at[n, h, way], device(to, y, z, a))

    def cf(n, h, o):
        ref = cg.at[a, at_x(o), slot(n), h]
        to = at_x(2 if n >= 2 else 1 if h == 0 else -1)
        return copy(ref, ref, cf_send.at[n, h], cf_recv.at[n, h], device(to, y, z, a))

    def pass_on(n, h, o):
        ref = cg.at[a, at_x(o), slot(n), h]
        copy(ref, ref, cc_send, cc_recv, other).start()

    def bx(i):
        to = at_x((1, -1, 2)[i])
        return copy(gb.at[x], gb.at[x], bx_send.at[i], bx_recv.at[i], device(to, y, z, a))

    def by(w, h):
        half = pl.ds(2 * h, 2)
        return copy(
            gb.at[half], cgb.at[b, p, half], by_send.at[w, h], by_recv.at[w, h],
            device(x, 2 * at_p(to_p[w]) + a, z, b),
        )

    def bw(w, h):
        ref = cgb.at[a, slot(w), pl.ds(2 * h, 2)]
        to = 2 * at_p(1 if w == 0 else -1) + b
        return copy(ref, ref, bw_send.at[w, h], bw_recv.at[w, h], device(x, to, z, a))

    def pass_b(n, h):
        ref = cgb.at[a, slot(n), pl.ds(2 * h, 2)]
        copy(ref, ref, bc_send, bc_recv, other).start()

    def step_bx():
        for i in range(3):
            bx(i).wait_recv()
        for h in range(2):
            by(0, h).start()
            by(1, h).start()

        @pl.when(aligned)
        def _():
            cgb[a, p] = gb[...]
            pass_b(3, 0)
            pass_b(3, 1)

    def step_by(w, h):
        by(w, h).wait_recv()
        if w == h:
            bw(w, h).start()
        else:
            @pl.when(crossed)
            def _():
                bw(w, h).start()
        pass_b(w, h)

    def step_bw(h):
        half = pl.ds(2 * h, 2)
        took(cgb.at[a, slot(2), half], bw_recv.at[(1 - odd) * h, h])
        pass_b(2, h)

        @pl.when(crossed)
        def _():
            took(cgb.at[a, slot(3), half], bw_recv.at[1, h])
            pass_b(3, h)

    def have(n, h):
        cx(n, h, 0).start()
        cx(n, h, 1).start()
        if n >= 2:
            cf(n, h, 0).start()
        pass_on(n, h, 0)

    def step_y(w, h):
        cy(w, h).wait_recv()
        if w == h:
            cw(w, h).start()
        else:
            @pl.when(crossed)
            def _():
                cw(w, h).start()
        have(w, h)

    def step_w(h):
        ref = cg.at[a, x, slot(2), h]
        took(ref, cw_recv.at[(1 - odd) * h, h])
        have(2, h)

        @pl.when(crossed)
        def _():
            took(cg.at[a, x, slot(3), h], cw_recv.at[1, h])
            have(3, h)

    def step_x(n, h):
        cx(n, h, 0, -1).wait_recv()
        if h == 0 and n < 2:
            cf(n, h, -1).start()
        cx(n, h, 1, 1).wait_recv()
        if h == 1 and n < 2:
            cf(n, h, 1).start()
        pass_on(n, h, -1)
        pass_on(n, h, 1)

    def step_f(n, h):
        cf(n, h, 2).wait_recv()
        pass_on(n, h, 2)

    def step_z(i, k):
        dz(i, k).wait_recv()
        if i == 2:
            dz(4, k).start()
            if k == 0:
                dz(6, k).start()
        if i == 3:
            dz(5, k).start()
            if k == 1:
                dz(6, k).start()

    for h in range(2):
        cy(0, h).start()
        cy(1, h).start()
        if h == 0:
            for i in range(3):
                bx(i).start()

        @pl.when(aligned)
        def _():
            have(3, h)

        if h == 0:
            d1().start()

            @pl.when(crossed)
            def _():
                d2().start()

    @pl.when(aligned)
    def _():
        d2().wait_recv()

    @pl.when(crossed)
    def _():
        took(dg.at[z, 0], d1_recv.at[0])
        took(dg.at[z, 1], d1_recv.at[1])

    for k in range(2):
        for i in range(4):
            dz(i, k).start()

    step_y(0, 0)
    step_y(1, 0)

    @pl.when(aligned)
    def _():
        step_x(3, 0)

    step_y(0, 1)
    step_y(1, 1)
    step_bx()

    @pl.when(aligned)
    def _():
        step_x(3, 1)
        step_f(3, 0)
        step_f(3, 1)

    step_w(0)
    for i in range(4):
        step_z(i, 0)
    step_x(0, 0)
    step_x(1, 0)
    step_w(1)
    for h in range(2):
        step_by(0, h)
        step_by(1, h)
    step_x(0, 1)
    step_x(1, 1)
    for i in range(4):
        step_z(i, 1)
    step_f(0, 0)
    step_f(1, 0)
    step_x(2, 0)

    @pl.when(crossed)
    def _():
        step_x(3, 0)

    step_bw(0)
    step_f(0, 1)
    step_f(1, 1)
    step_x(2, 1)

    @pl.when(crossed)
    def _():
        step_x(3, 1)

    for k in range(2):
        for i in range(4, 7):
            step_z(i, k)
    for h in range(2):
        step_f(2, h)

        @pl.when(crossed)
        def _():
            step_f(3, h)

    step_bw(1)
    dt[...] = dg[...].reshape(E, ND)
    for j in range(4):
        block = dt[:, pl.ds(128 * j, 128)].astype(F32)
        scale = 1.0 / jnp.sqrt(jnp.sum(block * block, axis=0, keepdims=True) * (1.0 / E) + 1e-06)
        xn[pl.ds(128 * j, 128), :] = (block * scale).T.astype(BF16)

    took(cg.at[0], cc_recv)
    took(cgb.at[0], bc_recv)

    ss[...] = jnp.zeros_like(ss)

    def unpack(t, _):
        xx, pp = lax.div(t, NP), lax.rem(t, NP)
        rows = pl.ds(pl.multiple_of(t * FL, FL), FL)
        for h in range(3):
            if h < 2:
                u0, u1, n = cg[0, xx, pp, h].astype(F32), cg[1, xx, pp, h].astype(F32), QA
            else:
                u0, u1, n = cgb[0, pp, xx].astype(F32), cgb[1, pp, xx].astype(F32), QB
            for g in range(2):
                part = jnp.concatenate([u0[FD * g:FD * g + FD], u1[FD * g:FD * g + FD]], axis=0)
                cols = pl.ds(2 * QA * h + n * g, n)
                ct[rows, cols] = part.astype(BF16)
                ss[:, cols] += jnp.sum((part * part).reshape(FL // 8, 8, n), axis=0)
        return 0

    lax.fori_loop(0, NX * NP, unpack, 0)

    rr[...] = jnp.zeros_like(rr)
    T = 256

    def scores(n, _):
        cols = pl.ds(pl.multiple_of(n * T, T), T)
        norm = jnp.sqrt(jnp.sum(ss[:, cols], axis=0, keepdims=True) * (1.0 / E) + 1e-06)
        s = jnp.dot(xn[...], ct[:, cols], preferred_element_type=F32)
        k = jnp.exp(s * (1.0 / (E * 0.02 * norm)))
        kk[:, cols] = k
        rr[...] += k[:, 0:128] + k[:, 128:256]
        return 0

    lax.fori_loop(0, NV // T, scores, 0, unroll=4)

    def reduce_leaf(i):
        pbuf[i, mine_leaf] = jnp.sum(rr[...].T, axis=0, keepdims=True)

        def send(j, _):
            ref = pbuf.at[i, mine_leaf]
            copy(ref, ref, p_send.at[i], p_recv.at[i], leaf_peer(j)).start()
            return 0

        lax.fori_loop(1, NL, send, 0)
        took(pbuf.at[i, pl.ds(0, NL - 1)], p_recv.at[i])
        u = 1.0 / jnp.sum(pbuf[i], axis=0)
        ub[...] = jnp.broadcast_to(u, (128, ND)).T

    def columns(i):
        def one(n, _):
            cols = pl.ds(pl.multiple_of(n * 128, 128), 128)
            w = kk[:, cols] * ub[...]
            if i == 1:
                ww[:, cols] = w.astype(BF16)
            total = jnp.sum(jnp.sum(w.reshape(ND // 8, 8, 128), axis=0), axis=0, keepdims=True)
            xbuf[i, x, :, cols] = total
            return 0

        lax.fori_loop(0, NV // 128, one, 0, unroll=2)

    def send_x(i):
        def send(j, _):
            copy(xbuf.at[i, x], xbuf.at[i, x], x_send.at[i], x_recv.at[i], x_peer(j)).start()
            return 0

        lax.fori_loop(1, NX, send, 0)

    def send_y(i):
        took(xbuf.at[i, pl.ds(0, NX - 1)], x_recv.at[i])
        ybuf[i, mine_doc] = jnp.sum(xbuf[i], axis=0)

        def send(j, _):
            ref = ybuf.at[i, mine_doc]
            copy(ref, ref, y_send.at[i], y_recv.at[i], doc_peer(j)).start()
            return 0

        lax.fori_loop(1, NY, send, 0)

    def take_y(i):
        took(ybuf.at[i, pl.ds(0, NY - 1)], y_recv.at[i])
        vv[...] = RATIO / jnp.sum(ybuf[i], axis=0)

    reduce_leaf(0)
    columns(0)
    send_x(0)
    send_y(0)
    take_y(0)

    rr[...] = jnp.zeros_like(rr)

    def rows_of(n, _):
        cols = pl.ds(pl.multiple_of(n * 128, 128), 128)
        rr[...] += kk[:, cols] * vv[:, cols]
        return 0

    lax.fori_loop(0, NV // 128, rows_of, 0, unroll=4)
    reduce_leaf(1)
    columns(1)
    send_x(1)

    XSEQ = (2, 1, -1, 0)

    def products(i):
        xx = at_x(XSEQ[i])
        rows = pl.ds(pl.multiple_of(xx * 192, 192), 192)
        gs[...] = jnp.dot(dt[rows, :], ww[...], preferred_element_type=F32)
        for yy in range(NY):
            r = FD * yy
            for h in range(2):
                at = 2 * Q * h
                unit = jnp.concatenate([gs[r:r + FD, at:at + Q], gs[r:r + FD, at + Q:at + 2 * Q]], axis=0)
                og[yy % 2, xx, yy // 2, h] = unit.astype(BF16)
        across(i).start()

    def across(i):
        xx = at_x(XSEQ[i])
        return copy(og.at[1 - a, xx], rc.at[xx], rk_send.at[i], rk_recv.at[i], other)

    def add(o, n, h, *others):
        ref = og.at[a, at_x(o), slot(n), h]
        total = ref[...].astype(F32) + rc[at_x(o), slot(n), h].astype(F32)
        for one in others:
            total = total + one.astype(F32)
        return ref, total

    def ra_first(n, h):
        to = at_x(1 if h == 0 else -1)
        return copy(
            og.at[a, at_x(2), slot(n), h], ra1.at[n, h], ra1_send.at[n, h], ra1_recv.at[n, h],
            device(to, y, z, a),
        )

    def ra_second(n, h, way):
        to = at_x(1 if way == 0 else -1)
        return copy(
            og.at[a, to, slot(n), h], ra2.at[way, n, h], ra2_send.at[way, n, h], ra2_recv.at[way, n, h],
            device(to, y, z, a),
        )

    def tf(w, n, h):
        to = 2 * at_p(2 * w - 1) + b
        return copy(og.at[a, x, slot(n), h], rf.at[w, h], tf_send.at[n - 2, h], tf_recv.at[w, h], device(x, to, z, a))

    def ty(n, h):
        return copy(
            og.at[a, x, slot(n), h], rt.at[n, h], ty_send.at[n, h], ty_recv.at[n, h],
            device(x, 2 * slot(n) + a, z, b),
        )

    def step_first():
        for n in ORDER:
            for h in range(2):
                ref, total = add(2, n, h)
                ref[...] = total.astype(BF16)
                ra_first(n, h).start()

    def step_plain(way):
        for n in ORDER:
            for h in range(2):
                if h != way:
                    ref, total = add(1 if way == 0 else -1, n, h)
                    ref[...] = total.astype(BF16)
                    ra_second(n, h, way).start()

    def step_joined(n, h):
        ra_first(n, h).wait_recv()
        ref, total = add(1 if h == 0 else -1, n, h, ra1[n, h])
        ref[...] = total.astype(BF16)
        ra_second(n, h, h).start()

    def step_home(n, h):
        ra_second(n, h, 0).wait_recv()
        ra_second(n, h, 1).wait_recv()
        ref, total = add(0, n, h, ra2[0, n, h], ra2[1, n, h])
        at = 2 * Q * h
        low = total[0:FD] * (vv[:, at:at + Q] * (1.0 / RATIO))
        high = total[FD:2 * FD] * (vv[:, at + Q:at + 2 * Q] * (1.0 / RATIO))
        total = jnp.concatenate([low, high], axis=0)
        if n < 2:
            if n == h:
                tf(n, 2, h).wait_recv()
            else:
                @pl.when(crossed)
                def _():
                    tf(n, 2, h).wait_recv()
            total = total + rf[n, h].astype(F32)
        ref[...] = total.astype(BF16)
        if n < 2:
            ty(n, h).start()
        if n == 2:
            tf((1 - odd) * h, n, h).start()
        if n == 3:
            @pl.when(crossed)
            def _():
                tf(1, n, h).start()

            @pl.when(aligned)
            def _():
                rt[2, h] = ref[...]

    @pl.when(aligned)
    def _():
        rf[0, 1] = jnp.zeros((2 * FD, Q), BF16)
        rf[1, 0] = jnp.zeros((2 * FD, Q), BF16)

    @pl.when(crossed)
    def _():
        rt[2] = jnp.zeros((2, 2 * FD, Q), BF16)

    H = ND // 2

    def turn(n, _):
        at = pl.ds(pl.multiple_of(n * 128, 128), 128)
        wt[at, :] = ww[:, at].T
        return 0

    def qz(h, i):
        to, o = BACK[i] if i < 2 else LAST_BACK[h]
        return copy(
            qq.at[h, at_z(o)], sq.at[h, i], q_send.at[h, i], q_recv.at[h, i], device(x, y, at_z(to), a)
        )

    def q_home(h, o, e):
        to = device(x, 2 * p + a, at_z(o), e)
        copy(qq.at[h, at_z(o), e], rp.at[h, 2 * (o + 2) + b], qh_send.at[h], qh_recv.at[h], to).start()

    def send_home(h, o):
        q_home(h, o, 1 - a)
        if o:
            q_home(h, o, a)
        else:
            @pl.when(crossed)
            def _():
                q_home(h, o, a)

            @pl.when(aligned)
            def _():
                rp[h, 2 * (o + 2) + b] = qq[h, z, a]

    def recon(targets, at):
        for i, o in enumerate(targets):
            rows = pl.ds(pl.multiple_of(at_z(o) * 2 * FL, 2 * FL), 2 * FL)
            r = at + 2 * FL * i
            cv[r:r + 2 * FL, :] = (ct[rows, :].astype(F32) * vv[...]).astype(BF16)
        part = jnp.dot(cv[at:at + 2 * FL * len(targets), :], wt[...], preferred_element_type=F32)
        for i, o in enumerate(targets):
            for e in range(2):
                r = (2 * i + e) * FL
                for h in range(2):
                    qq[h, at_z(o), e] = part[r:r + FL, h * H:(h + 1) * H].astype(BF16)

    def step_q(h):
        for w, o in enumerate((2, -2)):
            ref = qq.at[h, at_z(o)]
            qz(h, w).wait_recv()
            total = ref[...].astype(F32) + sq[h, w].astype(F32)
            if w == h:
                qz(h, 2).wait_recv()
                total = total + sq[h, 2].astype(F32)
            ref[...] = total.astype(BF16)
            send_home(h, o)

    def wait_home(h, sem):
        @pl.when(crossed)
        def _():
            took(rp.at[h], sem.at[h])

        @pl.when(aligned)
        def _():
            took(rp.at[h, pl.ds(0, 9)], sem.at[h])

    def last_q(h):
        wait_home(h, qh_recv)
        cols = slice(h * H, (h + 1) * H)
        back = rp[h, 0].astype(F32)
        for i in range(1, 10):
            back = back + rp[h, i].astype(F32)
        res_ref[:, cols] = (docs_ref[:, cols].astype(F32) - back).astype(BF16)

    products(0)
    products(1)
    across(0).wait_recv()
    step_first()
    products(2)
    send_y(1)
    lax.fori_loop(0, NV // 128, turn, 0, unroll=2)
    across(1).wait_recv()
    step_plain(0)
    products(3)
    across(2).wait_recv()
    step_plain(1)
    for n in (2, 3):
        step_joined(n, 0)
        step_joined(n, 1)
    across(3).wait_recv()
    for i in range(4):
        across(i).wait_send()
    take_y(1)
    recon((4, 3, -3), 0)
    for h in range(2):
        for i in (2, 0, 1):
            qz(h, i).start()
    for n in (0, 1):
        step_joined(n, 0)
        step_joined(n, 1)
    recon((2, -2, 1, -1, 0), 6 * FL)
    for h in range(2):
        for o in (1, -1, 0):
            send_home(h, o)
    for h in range(2):
        step_home(2, h)
    for h in range(2):
        step_home(3, h)
    step_q(0)
    step_q(1)
    step_home(0, 0)
    step_home(1, 0)
    step_home(0, 1)
    step_home(1, 1)

    for h in range(2):
        total = rt[2, h].astype(F32)
        for n in range(2):
            ty(n, h).wait_recv()
            total = total + rt[n, h].astype(F32)
        at = 2 * Q * h
        means_ref[:, at:at + Q] = total[0:FD].astype(BF16)
        means_ref[:, at + Q:at + 2 * Q] = total[FD:2 * FD].astype(BF16)

    last_q(0)
    last_q(1)

    d1().wait_send()

    @pl.when(crossed)
    def _():
        d2().wait_send()
        cw(0, 1).wait_send()
        cw(1, 0).wait_send()
        bw(0, 1).wait_send()
        bw(1, 0).wait_send()
        for h in range(2):
            tf(1, 3, h).wait_send()

    for h in range(2):
        cw(h, h).wait_send()
        bw(h, h).wait_send()
        tf(0, 2, h).wait_send()
        wait_home(h, qh_send)
        for i in range(7):
            if i < 3:
                qz(h, i).wait_send()
            dz(i, h).wait_send()
        for n in range(4):
            if n < 2:
                cy(n, h).wait_send()
                by(n, h).wait_send()
                ty(n, h).wait_send()
            cf(n, h, 0).wait_send()
            ra_first(n, h).wait_send()
            for way in range(2):
                cx(n, h, way).wait_send()
                ra_second(n, h, way).wait_send()
    for i in range(3):
        bx(i).wait_send()
    took(cg.at[0], cc_send)
    took(cgb.at[0], bc_send)
    for i in range(2):
        took(pbuf.at[i, pl.ds(0, NL - 1)], p_send.at[i])
        took(ybuf.at[i, pl.ds(0, NY - 1)], y_send.at[i])
        took(xbuf.at[i, pl.ds(0, NX - 1)], x_send.at[i])


def body(docs, centroids):
    dma = pltpu.SemaphoreType.DMA
    unit = (2 * FD, Q)
    residual, means = pl.pallas_call(
        kernel,
        out_shape=(jax.ShapeDtypeStruct((FL, ND), BF16), jax.ShapeDtypeStruct((FD, NV), BF16)),
        in_specs=[pl.BlockSpec(memory_space=pltpu.VMEM)] * 2,
        out_specs=(pl.BlockSpec(memory_space=pltpu.VMEM),) * 2,
        scratch_shapes=[
            pltpu.VMEM((2, 2 * FD, QA), BF16),
            pltpu.VMEM((NX, 2 * FD, QB), BF16),
            pltpu.VMEM((NZ, 2, FL, ND), BF16),
            pltpu.VMEM((2, NX, NP, 2, 2 * FD, QA), BF16),
            pltpu.VMEM((2, NP, NX, 2 * FD, QB), BF16),
            pltpu.VMEM((E, NV), BF16),
            pltpu.VMEM((ND, E), BF16),
            pltpu.VMEM((E, ND), BF16),
            pltpu.VMEM((ND, NV), F32),
            pltpu.VMEM((ND, NV), BF16),
            pltpu.VMEM((8, NV), F32),
            pltpu.VMEM((ND, 128), F32),
            pltpu.VMEM((ND, 128), F32),
            pltpu.VMEM((2, NL, 1, ND), F32),
            pltpu.VMEM((2, NY, 1, NV), F32),
            pltpu.VMEM((2, NX, 1, NV), F32),
            pltpu.VMEM((NV, ND), BF16),
            pltpu.VMEM((E, NV), BF16),
            pltpu.VMEM((192, NV), F32),
            pltpu.VMEM((2, NX, NP, 2, *unit), BF16),
            pltpu.VMEM((NX, NP, 2, *unit), BF16),
            pltpu.VMEM((NP, 2, *unit), BF16),
            pltpu.VMEM((2, NP, 2, *unit), BF16),
            pltpu.VMEM((2, 2, *unit), BF16),
            pltpu.VMEM((3, 2, *unit), BF16),
            pltpu.VMEM((2, NZ, 2, FL, ND // 2), BF16),
            pltpu.VMEM((2, 3, 2, FL, ND // 2), BF16),
            pltpu.VMEM((2, 10, FL, ND // 2), BF16),
            pltpu.VMEM((1, NV), F32),
            dma, dma((2,)), dma, dma, dma((7, 2)), dma((7, 2)),
            dma((3,)), dma((3,)), dma((2, 2)), dma((2, 2)), dma((2, 2)), dma((2, 2)), dma, dma,
            dma((2, 2)), dma((2, 2)), dma((2, 2)), dma((2, 2)), dma((NP, 2, 2)), dma((NP, 2, 2)), dma((NP, 2)), dma((NP, 2)), dma, dma,
            dma((2,)), dma((2,)), dma((2,)), dma((2,)), dma((2,)), dma((2,)),
            dma((4,)), dma((4,)), dma((NP, 2)), dma((NP, 2)), dma((2, NP, 2)), dma((2, NP, 2)),
            dma((2, 2)), dma((2, 2)), dma((2, 2)), dma((2, 2)),
            dma((2, 3)), dma((2, 3)), dma((2,)), dma((2,)),
        ],
        compiler_params=pltpu.CompilerParams(
            collective_id=0, has_side_effects=True, vmem_limit_bytes=48 * 2**20
        ),
        cost_estimate=pl.CostEstimate(
            flops=6 * ND * NV * E, bytes_accessed=2 * (ND * FL + NV * FD) * 2, transcendentals=ND * NV
        ),
    )(docs.T, centroids.T)
    return residual.T, means.T


def solution(mesh):
    return jax.shard_map(
        body,
        mesh=mesh,
        in_specs=(P("doc", "leaf"), P("leaf", "doc")),
        out_specs=(P("doc", "leaf"), P("leaf", "doc")),
        check_vma=False,
    )
```
